256 devices in a mesh: tile: 64 (over z, x_lo, y), head: 4 (over x_hi, core).
Axes of the slice: x: 4 (x_hi: 2, x_lo: 2; x = x_hi * 2 + x_lo), y: 4, z: 8, core: 2. Of those that a mesh axis runs over, the one named last changes fastest.
Arguments:
- query_vecs: bfloat16 [24576, 1536], P(('tile', 'head')), may hold values from -26 to 26
- key_vecs: bfloat16 [24576, 1536], P(('tile', 'head')), may hold values from -26 to 26
- value_vecs: bfloat16 [24576, 1536], P(('tile', 'head')), may hold values from -6 to 6
- outputs: bfloat16 [24576, 1536], P(('tile', 'head')), may hold values from -3 to 3
- out_grads: bfloat16 [24576, 1536], P(('tile', 'head')), may hold values from -6 to 6
- keep_mask: int32 [64, 27], P('tile'), may hold values from 0 to 1, as said below
Outputs:
- query_grads: bfloat16 [24576, 1536], P(('tile', 'head'))
- key_grads: bfloat16 [24576, 1536], P(('tile', 'head'))
- value_grads: bfloat16 [24576, 1536], P(('tile', 'head'))
The draws below stay inside these ranges and needn't reach their ends.
Inputs may be any that keep to these rules, and one draw needn't show every extreme that they name: `keep_mask`: entry 13 (the query tile itself) is 1 in every row.
All inputs are finite; a program needn't handle non-finite values.
Results may differ from the reference program's by a relative error of at most 0.0058.
Values may be sent and summed in bfloat16 or wider, within the bound.
A program may use at most 128 MiB of HBM per device.

```python
import jax
import jax.numpy as jnp
import numpy as np
from jax import lax

HEADS = 12
HDIM = 128
TT = 2
TILE = 384
WC = 8
HV = 4
NQT = 64
TOKENS = 24576
WIDTH = 1536


def common_rows(key):
    return jnp.clip(jax.random.normal(key, (TOKENS, WIDTH), jnp.float32), -4.0, 4.0)


def draw_query_vecs(key, part):
    key = jax.random.fold_in(key, 11)
    own_rows = jnp.clip(jax.random.normal(key, (TOKENS, WIDTH), jnp.float32), -4.0, 4.0)
    return own_rows.astype(jnp.bfloat16)


def draw_key_vecs(key, part):
    shared = common_rows(key)
    own_rows = shared
    return own_rows.astype(jnp.bfloat16)


def draw_keep_mask(key, part):
    key = jax.random.fold_in(key, 21)
    tile_ids = jnp.arange(NQT)
    level = 15 + 50 * tile_ids // NQT
    coins = jax.random.randint(key, (NQT, 27), 0, 100)
    kept = (coins < level[:, None]).astype(jnp.int32)
    center = jnp.arange(27) == 13
    return jnp.where(center[None, :], 1, kept).astype(jnp.int32)


def steps_of(stream_key, dims, split, smallest, high):
    factor_of = 1.0
    for position, parts in split:
        draws = jax.random.uniform(jax.random.fold_in(jax.random.fold_in(stream_key, 6), position), (parts,), jnp.float32, smallest / len(split), high / len(split))
        factor_of = factor_of * jnp.repeat(jnp.exp(draws), dims[position] // parts).reshape((-1,) + (1,) * (len(dims) - 1 - position))
    return factor_of


def normal_values(own_key, shape, scale, most, split=(), dtype=jnp.bfloat16):
    drawn = jax.random.normal(own_key, shape, jnp.float32) * scale
    if len(split) > 0:
        drawn = steps_of(own_key, shape, split, -0.22, 0.18) * drawn
    return jnp.clip(drawn, min=-most, max=most).astype(dtype)


def setup_inputs(seed: int = 0) -> dict:
    streams_of = jax.random.split(jax.random.key(seed), 7)
    return {
        "query_vecs": draw_query_vecs(jax.random.fold_in(streams_of[6], 71), 0),
        "key_vecs": draw_key_vecs(jax.random.fold_in(streams_of[6], 71), 0),
        "value_vecs": normal_values(streams_of[2], (TOKENS, WIDTH), 1.0, 6.0, ((0, 256),)),
        "outputs": normal_values(streams_of[3], (TOKENS, WIDTH), 0.5, 3.0, ((0, 256),)),
        "out_grads": normal_values(streams_of[4], (TOKENS, WIDTH), 1.0, 6.0, ((0, 256),)),
        "keep_mask": draw_keep_mask(jax.random.fold_in(streams_of[6], 71), 0),
    }


def rounded(array):
    return lax.optimization_barrier(array.astype(jnp.bfloat16)).astype(jnp.float32)


def reference(query_vecs, key_vecs, value_vecs, outputs, out_grads, keep_mask):
    score_scale = HDIM ** -0.5
    plane = HV * WC
    spots = np.arange(9)
    step_rows = spots // 3 - 1
    step_cols = spots % 3 - 1
    pool_spot = np.repeat(spots, TT)
    pool_time = np.tile(np.arange(TT), 9)

    def tiles_of(array):
        return array.reshape(NQT, TILE, HEADS, HDIM)

    queries, keys_all, values_all, outs_all, grads_all = [tiles_of(a) for a in (query_vecs, key_vecs, value_vecs, outputs, out_grads)]
    row_delta = jnp.einsum('nthd,nthd->nht', grads_all.astype(jnp.float32), outs_all.astype(jnp.float32))

    def window(tile_at):
        time_at = tile_at // plane
        height = (tile_at % plane) // WC
        width = tile_at % WC
        rows_two = height + jnp.asarray(step_rows[pool_spot], jnp.int32)
        cols_two = width + jnp.asarray(step_cols[pool_spot], jnp.int32)
        live = (rows_two >= 0) & (rows_two < HV) & (cols_two >= 0) & (cols_two < WC)
        ids = jnp.asarray(pool_time, jnp.int32) * plane + jnp.clip(rows_two, 0, HV - 1) * WC + jnp.clip(cols_two, 0, WC - 1)
        return time_at, ids.astype(jnp.int32), live

    def query_pass(tile_at):
        time_at, ids, live = window(tile_at)
        cols = ((jnp.asarray(pool_time, jnp.int32) - time_at + 1) * 9 + jnp.asarray(pool_spot, jnp.int32)).astype(jnp.int32)
        keep = (keep_mask[tile_at][cols] > 0) & live
        key_pool = keys_all[ids].astype(jnp.float32)
        value_pool = values_all[ids].astype(jnp.float32)
        scores = jnp.einsum('qhd,pkhd->hqpk', queries[tile_at].astype(jnp.float32), key_pool) * score_scale
        masked = jnp.where(keep[None, None, :, None], scores, -jnp.inf)
        row_top = jnp.max(masked, axis=(2, 3), keepdims=True)
        log_total = row_top + jnp.log(jnp.sum(jnp.exp(masked - row_top), axis=(2, 3), keepdims=True))
        weights = jnp.exp(masked - log_total)
        prob_grads = jnp.einsum('qhd,pkhd->hqpk', grads_all[tile_at].astype(jnp.float32), value_pool)
        score_grad = rounded(weights * (prob_grads - row_delta[tile_at][:, :, None, None]))
        query_grad = jnp.einsum('hqpk,pkhd->qhd', score_grad, key_pool) * score_scale
        return query_grad.astype(jnp.bfloat16), log_total[:, :, 0, 0]

    query_grad, log_totals = lax.map(query_pass, jnp.arange(NQT).astype(jnp.int32))

    def key_pass(tile_at):
        time_at, ids, live = window(tile_at)
        cols = ((time_at - jnp.asarray(pool_time, jnp.int32) + 1) * 9 + 8 - jnp.asarray(pool_spot, jnp.int32)).astype(jnp.int32)
        keep = (keep_mask[ids, cols] > 0) & live
        query_pool = queries[ids].astype(jnp.float32)
        grad_pool = grads_all[ids].astype(jnp.float32)
        lse_pool = jnp.transpose(log_totals[ids], (1, 0, 2))
        delta_pool = jnp.transpose(row_delta[ids], (1, 0, 2))
        scores = jnp.einsum('pqhd,khd->hpqk', query_pool, keys_all[tile_at].astype(jnp.float32)) * score_scale
        weights = jnp.exp(jnp.where(keep[None, :, None, None], scores, -jnp.inf) - lse_pool[..., None])
        value_term = rounded(jnp.einsum('hpqk,pqhd->pkhd', rounded(weights), grad_pool))
        prob_grads = jnp.einsum('pqhd,khd->hpqk', grad_pool, values_all[tile_at].astype(jnp.float32))
        score_grad = rounded(weights * (prob_grads - delta_pool[..., None]))
        key_term = rounded(jnp.einsum('hpqk,pqhd->pkhd', score_grad, query_pool) * score_scale)
        return jnp.sum(key_term, axis=0).astype(jnp.bfloat16), jnp.sum(value_term, axis=0).astype(jnp.bfloat16)

    key_grad, value_grad = lax.map(key_pass, jnp.arange(NQT).astype(jnp.int32))
    return (query_grad.reshape(TOKENS, WIDTH), key_grad.reshape(TOKENS, WIDTH), value_grad.reshape(TOKENS, WIDTH))
```

```python
import jax
import jax.numpy as jnp
from jax import lax
from jax.experimental import pallas as pl
from jax.experimental.pallas import tpu as pltpu
from jax.sharding import PartitionSpec as P

MESH = pl.DeviceIdType.MESH
HEADS = 12
HDIM = 128
PIECE = 96
PARTS = 4
TILE = PIECE * PARTS
WC = 8
ZC = 8
SCALE = HDIM**-0.5
LOG2E = 1.4426950408889634
F32 = jnp.float32
BF16 = jnp.bfloat16


def place():
    tile = lax.axis_index("tile")
    return tile // WC, tile % WC, lax.axis_index("head")


def item_here(z, g):
    r = (z - g - 1 + 2 * ZC) % ZC
    return r % 4 != 3, 3 * g + r % 4, r // 4


def item_z(head, half):
    return (head // 3 + 1 + head % 3 + 4 * half) % ZC


def greet(z, w, g):
    barrier = pltpu.get_barrier_semaphore()

    def hello(i, carry):
        zz, gg = i // PARTS, i % PARTS

        @pl.when(jnp.logical_or(zz != z, gg != g))
        def _():
            pl.semaphore_signal(barrier, inc=1, device_id=(zz * WC + w, gg), device_id_type=MESH)

        return carry

    lax.fori_loop(0, ZC * PARTS, hello, 0)

    @pl.when(w > 0)
    def _():
        pl.semaphore_signal(barrier, inc=1, device_id=(z * WC + w - 1, g), device_id_type=MESH)

    @pl.when(w < WC - 1)
    def _():
        pl.semaphore_signal(barrier, inc=1, device_id=(z * WC + w + 1, g), device_id_type=MESH)

    return barrier


def met(barrier, w):
    beside = jnp.where(jnp.logical_or(w == 0, w == WC - 1), 1, 2)
    pl.semaphore_wait(barrier, ZC * PARTS - 1 + beside)


def remote(src, dst, send_sem, recv_sem, tile, head):
    return pltpu.make_async_remote_copy(
        src_ref=src, dst_ref=dst, send_sem=send_sem, recv_sem=recv_sem, device_id=(tile, head), device_id_type=MESH
    )


def send(src, dst, send_sem, recv_sem, tile, head, own):
    @pl.when(own)
    def _():
        pltpu.make_async_copy(src, dst, recv_sem).start()

    @pl.when(jnp.logical_not(own))
    def _():
        remote(src, dst, send_sem, recv_sem, tile, head).start()


def sent(src, dst, send_sem, recv_sem, tile, head, own):
    @pl.when(jnp.logical_not(own))
    def _():
        remote(src, dst, send_sem, recv_sem, tile, head).wait_send()


def spread_kernel(
    q_ref, k_ref, v_ref, o_ref, g_ref, mask_ref,
    kv_ref, qg_ref, small_ref,
    kv_out, qg_out, small_out,
    kv_sent, kv2_sent, qg_sent, small_sent, kv_sem, qg_sem, small_sem, side_sent, side_sem,
):
    z, w, g = place()
    barrier = greet(z, w, g)
    busy, _, _ = item_here(z, g)
    t, h = z // 4, z % 4
    half = h // 2
    inner = jnp.logical_or(h == 1, h == 2)
    slot, slot2 = t * 3 + h - half, t * 3 + h - (1 - half)
    qslot = t * 2 + h % 2

    for j in range(HEADS):
        cols = slice(j * HDIM, (j + 1) * HDIM)
        kv_out[j, 0] = k_ref[:, cols]
        kv_out[j, 1] = v_ref[:, cols]
        qg_out[j, 0] = q_ref[:, cols]
        grad = g_ref[:, cols]
        qg_out[j, 1] = grad
        prod = grad.astype(F32) * o_ref[:, cols].astype(F32)
        prod = jnp.concatenate([prod, jnp.zeros((HDIM - PIECE, HDIM), F32)], axis=0)
        delta = jnp.sum(prod.T, axis=0, keepdims=True)
        small_out[j] = jnp.concatenate([delta, mask_ref[...], jnp.zeros((6, HDIM), F32)], axis=0)

    met(barrier, w)
    base = 3 * g + z

    def copies(s):
        j = (base + s) % HEADS
        zj, gj = item_z(j, half), j // 3
        own = jnp.logical_and(zj == z, gj == g)
        tile = zj * WC + w
        first = (
            (kv_out.at[j], kv_ref.at[1, slot, g], kv_sent.at[j], kv_sem.at[slot * PARTS + g], tile, gj, own),
            (qg_out.at[j], qg_ref.at[qslot, g], qg_sent.at[j], qg_sem.at[qslot * PARTS + g], tile, gj, own),
            (small_out.at[j], small_ref.at[qslot, g], small_sent.at[j], small_sem.at[qslot * PARTS + g], tile, gj, own),
        )
        z2 = item_z(j, 1 - half)
        own2 = jnp.logical_and(z2 == z, gj == g)
        second = (
            kv_out.at[j], kv_ref.at[1, slot2, g], kv2_sent.at[j], kv_sem.at[slot2 * PARTS + g], z2 * WC + w, gj, own2,
        )
        return first, second

    def start(s, carry):
        first, second = copies(s)
        send(*first[0])

        @pl.when(inner)
        def _():
            send(*second)

        send(*first[1])
        send(*first[2])
        return carry

    lax.fori_loop(0, HEADS, start, 0)

    def to_side(i, side):
        p, c = i // PARTS, i % PARTS
        step = 2 * side - 1
        return remote(
            kv_ref.at[1, p, c], kv_ref.at[2 - 2 * side, p, c], side_sent.at[side, i], side_sem.at[1 - side, i],
            z * WC + w + step, g,
        )

    def from_side(i, side):
        p, c = i // PARTS, i % PARTS
        return pltpu.make_async_copy(kv_ref.at[2 * side, p, c], kv_ref.at[2 * side, p, c], side_sem.at[side, i])

    @pl.when(busy)
    def _():
        def forward(i, carry):
            p, c = i // PARTS, i % PARTS
            pltpu.make_async_copy(kv_ref.at[1, p, c], kv_ref.at[1, p, c], kv_sem.at[i]).wait()

            @pl.when(w > 0)
            def _():
                to_side(i, 0).start()

            @pl.when(w < WC - 1)
            def _():
                to_side(i, 1).start()

            return carry

        lax.fori_loop(0, 6 * PARTS, forward, 0)

        def arrive(i, carry):
            p, c = i // PARTS, i % PARTS
            pltpu.make_async_copy(qg_ref.at[p, c], qg_ref.at[p, c], qg_sem.at[i]).wait()
            pltpu.make_async_copy(small_ref.at[p, c], small_ref.at[p, c], small_sem.at[i]).wait()
            return carry

        lax.fori_loop(0, 4 * PARTS, arrive, 0)

        def sides(i, carry):
            @pl.when(w > 0)
            def _():
                to_side(i, 0).wait_send()
                from_side(i, 0).wait()

            @pl.when(w < WC - 1)
            def _():
                to_side(i, 1).wait_send()
                from_side(i, 1).wait()

            return carry

        lax.fori_loop(0, 6 * PARTS, sides, 0)

    def finish(s, carry):
        first, second = copies(s)
        for copy in first:
            sent(*copy)

        @pl.when(inner)
        def _():
            sent(*second)

        return carry

    lax.fori_loop(0, HEADS, finish, 0)


def spread(q, k, v, o, g, mask):
    vmem = pl.BlockSpec(memory_space=pltpu.VMEM)
    hbm = pl.BlockSpec(memory_space=pl.ANY)
    sem = pltpu.SemaphoreType.DMA
    return pl.pallas_call(
        spread_kernel,
        out_shape=(
            jax.ShapeDtypeStruct((3, 6, PARTS, 2, PIECE, HDIM), BF16),
            jax.ShapeDtypeStruct((4, PARTS, 2, PIECE, HDIM), BF16),
            jax.ShapeDtypeStruct((4, PARTS, 8, HDIM), F32),
        ),
        in_specs=[vmem] * 6,
        out_specs=(hbm, hbm, hbm),
        scratch_shapes=[
            pltpu.VMEM((HEADS, 2, PIECE, HDIM), BF16),
            pltpu.VMEM((HEADS, 2, PIECE, HDIM), BF16),
            pltpu.VMEM((HEADS, 8, HDIM), F32),
            sem((HEADS,)),
            sem((HEADS,)),
            sem((HEADS,)),
            sem((HEADS,)),
            sem((6 * PARTS,)),
            sem((4 * PARTS,)),
            sem((4 * PARTS,)),
            sem((2, 6 * PARTS)),
            sem((2, 6 * PARTS)),
        ],
        compiler_params=pltpu.CompilerParams(
            collective_id=0, has_side_effects=True, vmem_limit_bytes=32 * 1024 * 1024
        ),
    )(q, k, v, o, g, mask)


def dot(a, b, dims):
    return lax.dot_general(a, b, (dims, ((), ())), preferred_element_type=F32)


def whole(ref):
    return ref[...].reshape(TILE, HDIM)


def attend_kernel(
    kv_ref, qg_ref, small_ref, mask_ref,
    dq_ref, own_ref, side_ref,
    weights, tops, top, total, query_t, key_t, terms,
):
    z, w, g = place()
    busy, _, half = item_here(z, g)

    @pl.when(busy)
    def _():
        def ready(n, carry):
            terms[n] = jnp.zeros((2, TILE, HDIM), F32)
            key_t[n] = kv_ref[n // 6, n % 6, :, 0].reshape(TILE, HDIM).T
            return carry

        lax.fori_loop(0, 18, ready, 0)

        def query(q, carry):
            t, row = q // 2, q % 2 + half
            queries = qg_ref[q, :, 0].reshape(TILE, HDIM)
            grads = qg_ref[q, :, 1].reshape(TILE, HDIM)
            delta = jnp.concatenate([small_ref[q, c, 0:1, :PIECE] for c in range(PARTS)], axis=1)
            top[...] = jnp.full((1, TILE), -jnp.inf, F32)
            total[...] = jnp.zeros((1, TILE), F32)
            query_t[...] = jnp.zeros((HDIM, TILE), F32)

            def kept(n):
                col, time2, row2 = n // 6, n % 6 // 3, n % 3
                up = row2 - row
                entry = (time2 - t + 1) * 9 + jnp.clip(up + 1, 0, 2) * 3 + col
                near = jnp.logical_and(up >= -1, up <= 1)
                there = jnp.logical_and(w + col >= 1, w + col <= WC)
                return jnp.logical_and(jnp.logical_and(near, there), mask_ref[q, entry] > 0)

            def scores(n, carry):
                @pl.when(kept(n))
                def _():
                    keys = kv_ref[n // 6, n % 6, :, 0].reshape(TILE, HDIM)
                    s = dot(keys, queries, ((1,), (1,))) * (SCALE * LOG2E)
                    before = top[...]
                    now = jnp.maximum(before, jnp.max(s, axis=0, keepdims=True))
                    e = jnp.exp2(s - now)
                    weights[n] = e
                    total[...] = total[...] * jnp.exp2(before - now) + jnp.sum(e, axis=0, keepdims=True)
                    top[...] = now
                    tops[n] = now

                return carry

            lax.fori_loop(0, 18, scores, 0)
            log_total = top[...] + jnp.log2(total[...])

            def grad_terms(n, carry):
                @pl.when(kept(n))
                def _():
                    values = kv_ref[n // 6, n % 6, :, 1].reshape(TILE, HDIM)
                    probs = weights[n] * jnp.exp2(tops[n] - log_total)
                    prob_grads = dot(values, grads, ((1,), (1,)))
                    score_grads = (probs * (prob_grads - delta)).astype(BF16)
                    terms[n, 0] += dot(score_grads, queries, ((1,), (0,)))
                    terms[n, 1] += dot(probs.astype(BF16), grads, ((1,), (0,)))
                    query_t[...] += dot(key_t[n], score_grads, ((1,), (0,)))

                return carry

            lax.fori_loop(0, 18, grad_terms, 0)
            dq_ref[q] = (query_t[...] * SCALE).astype(BF16).T.reshape(PARTS, PIECE, HDIM)
            return carry

        lax.fori_loop(0, 4, query, 0)

        def finish(p, carry):
            for kind, scale in ((0, SCALE), (1, 1.0)):
                for side in (0, 1):
                    term = (terms[12 * side + p, kind] * scale).astype(BF16)
                    side_ref[side, p, :, kind] = term.reshape(PARTS, PIECE, HDIM)
                own_ref[p, :, kind] = (terms[6 + p, kind] * scale).reshape(PARTS, PIECE, HDIM)
            return carry

        lax.fori_loop(0, 6, finish, 0)


def attend(kv, qg, small, mask):
    vmem = pl.BlockSpec(memory_space=pltpu.VMEM)
    return pl.pallas_call(
        attend_kernel,
        out_shape=(
            jax.ShapeDtypeStruct((4, PARTS, PIECE, HDIM), BF16),
            jax.ShapeDtypeStruct((6, PARTS, 2, PIECE, HDIM), F32),
            jax.ShapeDtypeStruct((2, 6, PARTS, 2, PIECE, HDIM), BF16),
        ),
        in_specs=[vmem, vmem, vmem, pl.BlockSpec(memory_space=pltpu.SMEM)],
        out_specs=(vmem, vmem, vmem),
        scratch_shapes=[
            pltpu.VMEM((18, TILE, TILE), F32),
            pltpu.VMEM((18, 1, TILE), F32),
            pltpu.VMEM((1, TILE), F32),
            pltpu.VMEM((1, TILE), F32),
            pltpu.VMEM((HDIM, TILE), F32),
            pltpu.VMEM((18, HDIM, TILE), BF16),
            pltpu.VMEM((18, 2, TILE, HDIM), F32),
        ],
        compiler_params=pltpu.CompilerParams(vmem_limit_bytes=56 * 1024 * 1024),
        cost_estimate=pl.CostEstimate(flops=12_000_000_000, bytes_accessed=10_000_000, transcendentals=9_000_000),
    )(kv, qg, small, mask)


def collect_kernel(
    dq_ref, own_ref, side_ref,
    oq_ref, ok_ref, ov_ref,
    beside, ready, got_q, got_kv,
    side_sent, side_sem, q_sent, q_sem, kv_sent, kv_sem,
):
    z, w, g = place()
    barrier = greet(z, w, g)
    busy, head, half = item_here(z, g)
    h = z % 4
    inner = jnp.logical_or(h == 1, h == 2)

    @pl.when(w == 0)
    def _():
        beside[0] = jnp.zeros(beside.shape[1:], BF16)

    @pl.when(w == WC - 1)
    def _():
        beside[1] = jnp.zeros(beside.shape[1:], BF16)

    met(barrier, w)

    def to_side(p, side):
        step = 2 * side - 1
        return remote(
            side_ref.at[side, p], beside.at[1 - side, p], side_sent.at[side, p], side_sem.at[1 - side, p],
            z * WC + w + step, g,
        )

    def from_side(p, side):
        return pltpu.make_async_copy(beside.at[side, p], beside.at[side, p], side_sem.at[side, p])

    def q_copy(i):
        n = (i + 4 * z) % (4 * PARTS)
        q, c = n // PARTS, n % PARTS
        to = q // 2 * 4 + 2 * half + q % 2
        own = jnp.logical_and(to == z, c == g)
        return dq_ref.at[q, c], got_q.at[head], q_sent.at[n], q_sem.at[head], to * WC + w, c, own

    def kv_copy(p, c):
        to = p // 3 * 4 + p % 3 + half
        other = jnp.where(to % 4 // 2 == half, 0, 1)
        own = jnp.logical_and(to == z, c == g)
        return (
            ready.at[p, c], got_kv.at[other, head], kv_sent.at[p * PARTS + c], kv_sem.at[other * HEADS + head],
            to * WC + w, c, own,
        )

    @pl.when(busy)
    def _():
        def start(s, carry):
            p = (s + z) % 6

            @pl.when(w > 0)
            def _():
                to_side(p, 0).start()

            @pl.when(w < WC - 1)
            def _():
                to_side(p, 1).start()

            return carry

        lax.fori_loop(0, 6, start, 0)

        def start_q(i, carry):
            send(*q_copy(i))
            return carry

        lax.fori_loop(0, 4 * PARTS, start_q, 0)

        def add(s, carry):
            p = (s + z) % 6

            @pl.when(w > 0)
            def _():
                from_side(p, 0).wait()

            @pl.when(w < WC - 1)
            def _():
                from_side(p, 1).wait()

            for c in range(PARTS):
                both = own_ref[p, c] + beside[0, p, c].astype(F32) + beside[1, p, c].astype(F32)
                ready[p, c] = both.astype(BF16)
                send(*kv_copy(p, c))
            return carry

        lax.fori_loop(0, 6, add, 0)

        def finish(p, carry):
            @pl.when(w > 0)
            def _():
                to_side(p, 0).wait_send()

            @pl.when(w < WC - 1)
            def _():
                to_side(p, 1).wait_send()

            for c in range(PARTS):
                sent(*kv_copy(p, c))
            return carry

        lax.fori_loop(0, 6, finish, 0)

        def finish_q(i, carry):
            sent(*q_copy(i))
            return carry

        lax.fori_loop(0, 4 * PARTS, finish_q, 0)

    def arrived(j, carry):
        pltpu.make_async_copy(got_q.at[j], got_q.at[j], q_sem.at[j]).wait()
        pltpu.make_async_copy(got_kv.at[0, j], got_kv.at[0, j], kv_sem.at[j]).wait()

        @pl.when(inner)
        def _():
            pltpu.make_async_copy(got_kv.at[1, j], got_kv.at[1, j], kv_sem.at[HEADS + j]).wait()

        return carry

    lax.fori_loop(0, HEADS, arrived, 0)
    for j in range(HEADS):
        oq_ref[:, j * HDIM : (j + 1) * HDIM] = got_q[j]

    @pl.when(inner)
    def _():
        for j in range(HEADS):
            both = (got_kv[0, j].astype(F32) + got_kv[1, j].astype(F32)).astype(BF16)
            ok_ref[:, j * HDIM : (j + 1) * HDIM] = both[0]
            ov_ref[:, j * HDIM : (j + 1) * HDIM] = both[1]

    @pl.when(jnp.logical_not(inner))
    def _():
        for j in range(HEADS):
            ok_ref[:, j * HDIM : (j + 1) * HDIM] = got_kv[0, j, 0]
            ov_ref[:, j * HDIM : (j + 1) * HDIM] = got_kv[0, j, 1]


def collect(dq, own, side):
    vmem = pl.BlockSpec(memory_space=pltpu.VMEM)
    hbm = pl.BlockSpec(memory_space=pl.ANY)
    sem = pltpu.SemaphoreType.DMA
    out = jax.ShapeDtypeStruct((PIECE, HEADS * HDIM), BF16)
    return pl.pallas_call(
        collect_kernel,
        out_shape=(out, out, out),
        in_specs=[hbm, vmem, hbm],
        out_specs=(vmem, vmem, vmem),
        scratch_shapes=[
            pltpu.VMEM((2, 6, PARTS, 2, PIECE, HDIM), BF16),
            pltpu.VMEM((6, PARTS, 2, PIECE, HDIM), BF16),
            pltpu.VMEM((HEADS, PIECE, HDIM), BF16),
            pltpu.VMEM((2, HEADS, 2, PIECE, HDIM), BF16),
            sem((2, 6)),
            sem((2, 6)),
            sem((4 * PARTS,)),
            sem((HEADS,)),
            sem((6 * PARTS,)),
            sem((2 * HEADS,)),
        ],
        compiler_params=pltpu.CompilerParams(
            collective_id=1, has_side_effects=True, vmem_limit_bytes=32 * 1024 * 1024
        ),
    )(dq, own, side)


def shards(query_vecs, key_vecs, value_vecs, outputs, out_grads, keep_mask):
    mask = jnp.pad(keep_mask.astype(F32), ((0, 0), (0, HDIM - keep_mask.shape[1])))
    kv, qg, small = spread(query_vecs, key_vecs, value_vecs, outputs, out_grads, mask)
    kept = small[:, 0, 1, :].astype(jnp.int32)
    dq, own, side = attend(kv, qg, small, kept)
    return collect(dq, own, side)


def solution(mesh):
    rows = P(("tile", "head"), None)
    return jax.shard_map(
        shards,
        mesh=mesh,
        in_specs=(rows, rows, rows, rows, rows, P("tile", None)),
        out_specs=(rows, rows, rows),
        check_vma=False,
    )
```

```python
import jax
import jax.numpy as jnp
from jax import lax
from jax.experimental import pallas as pl
from jax.experimental.pallas import tpu as pltpu
from jax.sharding import PartitionSpec as P

MESH = pl.DeviceIdType.MESH
HEADS = 12
HDIM = 128
PIECE = 96
PARTS = 4
TILE = PIECE * PARTS
WC = 8
ZC = 8
SCALE = HDIM**-0.5
LOG2E = 1.4426950408889634
F32 = jnp.float32
BF16 = jnp.bfloat16


def place():
    tile = lax.axis_index("tile")
    return tile // WC, tile % WC, lax.axis_index("head")


def item_here(z, g):
    r = (z - 2 * (g // 2) + ZC) % ZC
    return r % 4 != 0, 6 * (g // 2) + r % 4 - 1 + 3 * (r // 4), g % 2


def item_z(head):
    k = head % 6
    return (k % 3 + 1 + 4 * (k // 3) + 2 * (head // 6)) % ZC


def greet(z, w, g):
    barrier = pltpu.get_barrier_semaphore()

    def hello(i, carry):
        zz, gg = i // PARTS, i % PARTS

        @pl.when(jnp.logical_or(zz != z, gg != g))
        def _():
            pl.semaphore_signal(barrier, inc=1, device_id=(zz * WC + w, gg), device_id_type=MESH)

        return carry

    lax.fori_loop(0, ZC * PARTS, hello, 0)

    @pl.when(w > 0)
    def _():
        pl.semaphore_signal(barrier, inc=1, device_id=(z * WC + w - 1, g), device_id_type=MESH)

    @pl.when(w < WC - 1)
    def _():
        pl.semaphore_signal(barrier, inc=1, device_id=(z * WC + w + 1, g), device_id_type=MESH)

    return barrier


def met(barrier, w):
    beside = jnp.where(jnp.logical_or(w == 0, w == WC - 1), 1, 2)
    pl.semaphore_wait(barrier, ZC * PARTS - 1 + beside)


def remote(src, dst, send_sem, recv_sem, tile, head):
    return pltpu.make_async_remote_copy(
        src_ref=src, dst_ref=dst, send_sem=send_sem, recv_sem=recv_sem, device_id=(tile, head), device_id_type=MESH
    )


def send(src, dst, send_sem, recv_sem, tile, head, own):
    @pl.when(own)
    def _():
        pltpu.make_async_copy(src, dst, recv_sem).start()

    @pl.when(jnp.logical_not(own))
    def _():
        remote(src, dst, send_sem, recv_sem, tile, head).start()


def sent(src, dst, send_sem, recv_sem, tile, head, own):
    @pl.when(jnp.logical_not(own))
    def _():
        remote(src, dst, send_sem, recv_sem, tile, head).wait_send()


def spread_kernel(
    q_ref, k_ref, v_ref, o_ref, g_ref, mask_ref,
    kv_ref, qg_ref, small_ref,
    given, kv_out, qg_out, small_out,
    given_sem, kv_sent, qg_sent, small_sent, kv_sem, qg_sem, small_sem, side_sent, side_sem, core_sent, core_sem,
):
    z, w, g = place()
    loads = [pltpu.make_async_copy(ref, given.at[i], given_sem.at[i]) for i, ref in enumerate((k_ref, v_ref, q_ref, g_ref, o_ref))]
    for load in loads:
        load.start()
    barrier = greet(z, w, g)
    busy, head, half = item_here(z, g)
    t, h = z // 4, z % 4
    to_half, qslot = h // 2, z // 4 * 2 + h % 2
    slot = t * 3 + h - to_half
    source = g * 4 + qslot
    base = 3 * source // 4

    for i, load in enumerate(loads[:2]):
        load.wait()
        for j in range(HEADS):
            kv_out[j, i] = given[i, :, j * HDIM : (j + 1) * HDIM]

    met(barrier, w)

    def target(s):
        j = (base + s) % HEADS
        zj, gj = item_z(j), 2 * (j // 6) + to_half
        return j, zj * WC + w, gj, jnp.logical_and(zj == z, gj == g)

    def kv_copy(s):
        j, tile, gj, own = target(s)
        return kv_out.at[j], kv_ref.at[1, slot, g], kv_sent.at[j], kv_sem.at[qslot * PARTS + g], tile, gj, own

    def qg_copy(s):
        j, tile, gj, own = target(s)
        return qg_out.at[j], qg_ref.at[qslot, g], qg_sent.at[j], qg_sem.at[qslot * PARTS + g], tile, gj, own

    def small_copy(s):
        j, tile, gj, own = target(s)
        return small_out.at[j], small_ref.at[qslot, g], small_sent.at[j], small_sem.at[qslot * PARTS + g], tile, gj, own

    def start_kv(s, carry):
        send(*kv_copy(s))
        return carry

    lax.fori_loop(0, HEADS, start_kv, 0)

    for load in loads[2:]:
        load.wait()
    for j in range(HEADS):
        cols = slice(j * HDIM, (j + 1) * HDIM)
        qg_out[j, 0] = given[2, :, cols]
        grad = given[3, :, cols]
        qg_out[j, 1] = grad
        prod = grad.astype(F32) * given[4, :, cols].astype(F32)
        prod = jnp.concatenate([prod, jnp.zeros((HDIM - PIECE, HDIM), F32)], axis=0)
        delta = jnp.sum(prod.T, axis=0, keepdims=True)
        small_out[j] = jnp.concatenate([delta, mask_ref[...], jnp.zeros((6, HDIM), F32)], axis=0)

    def start_qg(s, carry):
        send(*qg_copy(s))
        send(*small_copy(s))
        return carry

    lax.fori_loop(0, HEADS, start_qg, 0)

    def to_side(p, c, side):
        row = p // 2 * 3 + p % 2 + half
        i = p * PARTS + c
        return remote(
            kv_ref.at[1, row, c], kv_ref.at[2 - 2 * side, row, c], side_sent.at[side, i], side_sem.at[1 - side, i],
            z * WC + w + 2 * side - 1, g,
        )

    def to_core(p, c, col):
        i = p // 2 * PARTS + c
        return remote(
            kv_ref.at[col, p // 2 * 3 + 1, c], kv_ref.at[col, p // 2 * 3 + 2 * half, c],
            core_sent.at[col, i], core_sem.at[col, i], z * WC + w, g + 1 - 2 * half,
        )

    def here(ref, arrived_sem):
        return pltpu.make_async_copy(ref, ref, arrived_sem)

    def near(side):
        return w > 0 if side == 0 else w < WC - 1

    @pl.when(busy)
    def _():
        first = (4 * head + 3) // 3

        def forward(i, carry):
            lin = (first - i + 16) % 16
            c, p = lin // 4, lin % 4
            here(kv_ref.at[1, p // 2 * 3 + p % 2 + half, c], kv_sem.at[p * PARTS + c]).wait()
            for side in (0, 1):

                @pl.when(near(side))
                def _():
                    to_side(p, c, side).start()

            @pl.when(p % 2 + half == 1)
            def _():
                to_core(p, c, 1).start()

            return carry

        lax.fori_loop(0, 16, forward, 0)

        def side_in(i, carry):
            lin = (first - i + 16) % 16
            c, p = lin // 4, lin % 4
            for side in (0, 1):

                @pl.when(near(side))
                def _():
                    here(kv_ref.at[2 * side, p // 2 * 3 + p % 2 + half, c], side_sem.at[side, p * PARTS + c]).wait()

                    @pl.when(p % 2 + half == 1)
                    def _():
                        to_core(p, c, 2 * side).start()

            return carry

        lax.fori_loop(0, 16, side_in, 0)

        def arrive(i, carry):
            p, c = i // PARTS, i % PARTS
            here(qg_ref.at[p, c], qg_sem.at[i]).wait()
            here(small_ref.at[p, c], small_sem.at[i]).wait()
            for side in (0, 1):

                @pl.when(near(side))
                def _():
                    to_side(p, c, side).wait_send()

            return carry

        lax.fori_loop(0, 16, arrive, 0)

        def core_in(i, carry):
            p, c = i // PARTS * 2, i % PARTS

            def both(col):
                here(kv_ref.at[col, i // PARTS * 3 + 2 * (1 - half), c], core_sem.at[col, i]).wait()
                to_core(p, c, col).wait_send()

            both(1)
            for side in (0, 1):

                @pl.when(near(side))
                def _():
                    both(2 * side)

            return carry

        lax.fori_loop(0, 2 * PARTS, core_in, 0)

    def finish(s, carry):
        sent(*kv_copy(s))
        sent(*qg_copy(s))
        sent(*small_copy(s))
        return carry

    lax.fori_loop(0, HEADS, finish, 0)


def spread(q, k, v, o, g, mask):
    vmem = pl.BlockSpec(memory_space=pltpu.VMEM)
    hbm = pl.BlockSpec(memory_space=pl.ANY)
    sem = pltpu.SemaphoreType.DMA
    return pl.pallas_call(
        spread_kernel,
        out_shape=(
            jax.ShapeDtypeStruct((3, 6, PARTS, 2, PIECE, HDIM), BF16),
            jax.ShapeDtypeStruct((4, PARTS, 2, PIECE, HDIM), BF16),
            jax.ShapeDtypeStruct((4, PARTS, 8, HDIM), F32),
        ),
        in_specs=[hbm] * 5 + [vmem],
        out_specs=(hbm, hbm, hbm),
        scratch_shapes=[
            pltpu.VMEM((5, PIECE, HEADS * HDIM), BF16),
            pltpu.VMEM((HEADS, 2, PIECE, HDIM), BF16),
            pltpu.VMEM((HEADS, 2, PIECE, HDIM), BF16),
            pltpu.VMEM((HEADS, 8, HDIM), F32),
            sem((5,)),
            sem((HEADS,)),
            sem((HEADS,)),
            sem((HEADS,)),
            sem((16,)),
            sem((16,)),
            sem((16,)),
            sem((2, 16)),
            sem((2, 16)),
            sem((3, 2 * PARTS)),
            sem((3, 2 * PARTS)),
        ],
        compiler_params=pltpu.CompilerParams(
            collective_id=0, has_side_effects=True, vmem_limit_bytes=60 * 1024 * 1024
        ),
    )(q, k, v, o, g, mask)


def dot(a, b, dims):
    return lax.dot_general(a, b, (dims, ((), ())), preferred_element_type=F32)


def attend_kernel(
    kv_any, qg_any, small_any, mask_ref,
    dq_ref, own_ref, halo_ref, outer_ref, inner_ref,
    kv_ref, qg_ref, small_ref, load_sem, weights, tops, top, total, query_t, key_t, terms,
):
    z, w, g = place()
    busy, _, half = item_here(z, g)

    @pl.when(busy)
    def _():
        loads = [
            pltpu.make_async_copy(kv_any, kv_ref, load_sem.at[0]),
            pltpu.make_async_copy(qg_any, qg_ref, load_sem.at[1]),
            pltpu.make_async_copy(small_any, small_ref, load_sem.at[2]),
        ]
        for load in loads:
            load.start()
        for load in loads:
            load.wait()

        def ready(n, carry):
            terms[n] = jnp.zeros((2, TILE, HDIM), F32)
            key_t[n] = kv_ref[n // 6, n % 6, :, 0].reshape(TILE, HDIM).T
            return carry

        lax.fori_loop(0, 18, ready, 0)

        def query(q, carry):
            t, row = q // 2, q % 2 + half
            queries = qg_ref[q, :, 0].reshape(TILE, HDIM)
            grads = qg_ref[q, :, 1].reshape(TILE, HDIM)
            delta = jnp.concatenate([small_ref[q, c, 0:1, :PIECE] for c in range(PARTS)], axis=1)
            top[...] = jnp.full((1, TILE), -jnp.inf, F32)
            total[...] = jnp.zeros((1, TILE), F32)
            query_t[...] = jnp.zeros((HDIM, TILE), F32)

            def kept(n):
                col, time2, row2 = n // 6, n % 6 // 3, n % 3
                up = row2 - row
                entry = (time2 - t + 1) * 9 + jnp.clip(up + 1, 0, 2) * 3 + col
                near = jnp.logical_and(up >= -1, up <= 1)
                there = jnp.logical_and(w + col >= 1, w + col <= WC)
                return jnp.logical_and(jnp.logical_and(near, there), mask_ref[q, entry] > 0)

            def scores(n, carry):
                @pl.when(kept(n))
                def _():
                    keys = kv_ref[n // 6, n % 6, :, 0].reshape(TILE, HDIM)
                    s = dot(keys, queries, ((1,), (1,))) * (SCALE * LOG2E)
                    before = top[...]
                    now = jnp.maximum(before, jnp.max(s, axis=0, keepdims=True))
                    e = jnp.exp2(s - now)
                    weights[n] = e
                    total[...] = total[...] * jnp.exp2(before - now) + jnp.sum(e, axis=0, keepdims=True)
                    top[...] = now
                    tops[n] = now

                return carry

            lax.fori_loop(0, 18, scores, 0)
            log_total = top[...] + jnp.log2(total[...])

            def grad_terms(n, carry):
                @pl.when(kept(n))
                def _():
                    values = kv_ref[n // 6, n % 6, :, 1].reshape(TILE, HDIM)
                    probs = weights[n] * jnp.exp2(tops[n] - log_total)
                    prob_grads = dot(values, grads, ((1,), (1,)))
                    score_grads = (probs * (prob_grads - delta)).astype(BF16)
                    terms[n, 0] += dot(score_grads, queries, ((1,), (0,)))
                    terms[n, 1] += dot(probs.astype(BF16), grads, ((1,), (0,)))
                    query_t[...] += dot(key_t[n], score_grads, ((1,), (0,)))

                return carry

            lax.fori_loop(0, 18, grad_terms, 0)
            dq_ref[q] = (query_t[...] * SCALE).astype(BF16).T.reshape(PARTS, PIECE, HDIM)
            return carry

        lax.fori_loop(0, 4, query, 0)

        def finish(t, carry):
            for kind, scale in ((0, SCALE), (1, 1.0)):

                def term(col, row):
                    return (terms[6 * col + 3 * t + row, kind] * scale).reshape(PARTS, PIECE, HDIM)

                for col in range(3):
                    halo_ref[col, t, :, kind] = term(col, 2 * (1 - half)).astype(BF16)
                for side in (0, 1):
                    outer_ref[side, t, :, kind] = term(2 * side, 2 * half).astype(BF16)
                    inner_ref[side, t, :, kind] = term(2 * side, 1)
                for row in (0, 1):
                    own_ref[2 * t + row, :, kind] = term(1, row + half)
            return carry

        lax.fori_loop(0, 2, finish, 0)


def attend(kv, qg, small, mask):
    vmem = pl.BlockSpec(memory_space=pltpu.VMEM)
    hbm = pl.BlockSpec(memory_space=pl.ANY)
    block = (PARTS, 2, PIECE, HDIM)
    return pl.pallas_call(
        attend_kernel,
        out_shape=(
            jax.ShapeDtypeStruct((4, PARTS, PIECE, HDIM), BF16),
            jax.ShapeDtypeStruct((4, *block), F32),
            jax.ShapeDtypeStruct((3, 2, *block), BF16),
            jax.ShapeDtypeStruct((2, 2, *block), BF16),
            jax.ShapeDtypeStruct((2, 2, *block), F32),
        ),
        in_specs=[hbm, hbm, hbm, pl.BlockSpec(memory_space=pltpu.SMEM)],
        out_specs=(vmem,) * 5,
        scratch_shapes=[
            pltpu.VMEM(kv.shape, BF16),
            pltpu.VMEM(qg.shape, BF16),
            pltpu.VMEM(small.shape, F32),
            pltpu.SemaphoreType.DMA((3,)),
            pltpu.VMEM((18, TILE, TILE), F32),
            pltpu.VMEM((18, 1, TILE), F32),
            pltpu.VMEM((1, TILE), F32),
            pltpu.VMEM((1, TILE), F32),
            pltpu.VMEM((HDIM, TILE), F32),
            pltpu.VMEM((18, HDIM, TILE), BF16),
            pltpu.VMEM((18, 2, TILE, HDIM), F32),
        ],
        compiler_params=pltpu.CompilerParams(vmem_limit_bytes=60 * 1024 * 1024),
        cost_estimate=pl.CostEstimate(flops=12_000_000_000, bytes_accessed=10_000_000, transcendentals=9_000_000),
    )(kv, qg, small, mask)


def collect_kernel(
    dq_ref, own_any, halo_ref, outer_ref, inner_any,
    oq_ref, ok_ref, ov_ref,
    own_ref, inner_ref, from_core, mixed, beside, ready, got_q, got_kv,
    load_sem, core_sent, core_sem, side_sent, side_sem, q_sent, q_sem, kv_sent, kv_sem,
):
    z, w, g = place()
    loads = [
        pltpu.make_async_copy(inner_any, inner_ref, load_sem.at[0]),
        pltpu.make_async_copy(own_any, own_ref, load_sem.at[1]),
    ]
    for load in loads:
        load.start()
    barrier = greet(z, w, g)
    busy, head, half = item_here(z, g)

    @pl.when(w == 0)
    def _():
        beside[0] = jnp.zeros(beside.shape[1:], BF16)

    @pl.when(w == WC - 1)
    def _():
        beside[1] = jnp.zeros(beside.shape[1:], BF16)

    met(barrier, w)

    def near(side):
        return w > 0 if side == 0 else w < WC - 1

    def here(ref, arrived_sem):
        return pltpu.make_async_copy(ref, ref, arrived_sem)

    def to_core(t, col):
        return remote(
            halo_ref.at[col, t], from_core.at[col, t], core_sent.at[col, t], core_sem.at[col, t],
            z * WC + w, g + 1 - 2 * half,
        )

    def to_side(t, inner, side):
        p = 2 * t + (1 - half if inner else half)
        src = mixed.at[side, t] if inner else outer_ref.at[side, t]
        return remote(
            src, beside.at[1 - side, p], side_sent.at[side, p], side_sem.at[1 - side, p], z * WC + w + 2 * side - 1, g
        )

    def q_copy(i):
        n = (i + 4 * z) % (4 * PARTS)
        q, c = n // PARTS, n % PARTS
        to = q // 2 * 4 + 2 * half + q % 2
        own = jnp.logical_and(to == z, c == g)
        return dq_ref.at[q, c], got_q.at[head], q_sent.at[n], q_sem.at[head], to * WC + w, c, own

    def kv_copy(p, c):
        to = p // 2 * 4 + p % 2 + 2 * half
        own = jnp.logical_and(to == z, c == g)
        return ready.at[p, c], got_kv.at[head], kv_sent.at[p * PARTS + c], kv_sem.at[head], to * WC + w, c, own

    @pl.when(busy)
    def _():
        for col in (0, 2, 1):
            for t in (0, 1):

                @pl.when(near(col // 2) if col != 1 else w >= 0)
                def _():
                    to_core(t, col).start()

        for t in (0, 1):
            for side in (0, 1):

                @pl.when(near(side))
                def _():
                    to_side(t, False, side).start()

        def start_q(i, carry):
            send(*q_copy(i))
            return carry

        lax.fori_loop(0, 4 * PARTS, start_q, 0)
        for load in loads:
            load.wait()

        for t in (0, 1):
            for side in (0, 1):

                @pl.when(near(side))
                def _():
                    here(from_core.at[2 * side, t], core_sem.at[2 * side, t]).wait()
                    for c in range(PARTS):
                        both = inner_ref[side, t, c] + from_core[2 * side, t, c].astype(F32)
                        mixed[side, t, c] = both.astype(BF16)
                    to_side(t, True, side).start()

        for t in (0, 1):
            here(from_core.at[1, t], core_sem.at[1, t]).wait()
            p = 2 * t + 1 - half
            for c in range(PARTS):
                own_ref[p, c] = own_ref[p, c] + from_core[1, t, c].astype(F32)

        for inner in (False, True):

            def add(i, carry):
                t = (i + z // 4) % 2
                p = 2 * t + (1 - half if inner else half)
                for side in (0, 1):

                    @pl.when(near(side))
                    def _():
                        here(beside.at[side, p], side_sem.at[side, p]).wait()

                for c in range(PARTS):
                    both = own_ref[p, c] + beside[0, p, c].astype(F32) + beside[1, p, c].astype(F32)
                    ready[p, c] = both.astype(BF16)
                    send(*kv_copy(p, c))
                return carry

            lax.fori_loop(0, 2, add, 0)

        for t in (0, 1):
            to_core(t, 1).wait_send()
            for side in (0, 1):

                @pl.when(near(side))
                def _():
                    to_core(t, 2 * side).wait_send()
                    to_side(t, False, side).wait_send()
                    to_side(t, True, side).wait_send()

        def finish(n, carry):
            sent(*kv_copy(n // PARTS, n % PARTS))
            sent(*q_copy(n))
            return carry

        lax.fori_loop(0, 4 * PARTS, finish, 0)

    @pl.when(jnp.logical_not(busy))
    def _():
        for load in loads:
            load.wait()

    for j in range(HEADS):
        cols = slice(j * HDIM, (j + 1) * HDIM)
        here(got_q.at[j], q_sem.at[j]).wait()
        oq_ref[:, cols] = got_q[j]
        here(got_kv.at[j], kv_sem.at[j]).wait()
        ok_ref[:, cols] = got_kv[j, 0]
        ov_ref[:, cols] = got_kv[j, 1]


def collect(dq, own, halo, outer, inner):
    vmem = pl.BlockSpec(memory_space=pltpu.VMEM)
    hbm = pl.BlockSpec(memory_space=pl.ANY)
    sem = pltpu.SemaphoreType.DMA
    out = jax.ShapeDtypeStruct((PIECE, HEADS * HDIM), BF16)
    block = (PARTS, 2, PIECE, HDIM)
    return pl.pallas_call(
        collect_kernel,
        out_shape=(out, out, out),
        in_specs=[hbm] * 5,
        out_specs=(vmem, vmem, vmem),
        scratch_shapes=[
            pltpu.VMEM((4, *block), F32),
            pltpu.VMEM((2, 2, *block), F32),
            pltpu.VMEM((3, 2, *block), BF16),
            pltpu.VMEM((2, 2, *block), BF16),
            pltpu.VMEM((2, 4, *block), BF16),
            pltpu.VMEM((4, *block), BF16),
            pltpu.VMEM((HEADS, PIECE, HDIM), BF16),
            pltpu.VMEM((HEADS, 2, PIECE, HDIM), BF16),
            sem((2,)),
            sem((3, 2)),
            sem((3, 2)),
            sem((2, 4)),
            sem((2, 4)),
            sem((4 * PARTS,)),
            sem((HEADS,)),
            sem((4 * PARTS,)),
            sem((HEADS,)),
        ],
        compiler_params=pltpu.CompilerParams(
            collective_id=1, has_side_effects=True, vmem_limit_bytes=60 * 1024 * 1024
        ),
    )(dq, own, halo, outer, inner)


def shards(query_vecs, key_vecs, value_vecs, outputs, out_grads, keep_mask):
    mask = jnp.pad(keep_mask.astype(F32), ((0, 0), (0, HDIM - keep_mask.shape[1])))
    kv, qg, small = spread(query_vecs, key_vecs, value_vecs, outputs, out_grads, mask)
    kept = small[:, 0, 1, :].astype(jnp.int32)
    return collect(*attend(kv, qg, small, kept))


def solution(mesh):
    rows = P(("tile", "head"), None)
    return jax.shard_map(
        shards,
        mesh=mesh,
        in_specs=(rows, rows, rows, rows, rows, P("tile", None)),
        out_specs=(rows, rows, rows),
        check_vma=False,
    )
```

```python
import jax
import jax.numpy as jnp
from jax import lax
from jax.experimental import pallas as pl
from jax.experimental.pallas import tpu as pltpu
from jax.sharding import PartitionSpec as P

MESH = pl.DeviceIdType.MESH
HEADS = 12
HDIM = 128
PIECE = 96
PARTS = 4
TILE = PIECE * PARTS
WC = 8
GROUPS = (4, 3, 2, 1)
ZC = 8
SCALE = HDIM**-0.5
LOG2E = 1.4426950408889634
F32 = jnp.float32
BF16 = jnp.bfloat16


def place():
    tile = lax.axis_index("tile")
    return tile // WC, tile % WC, lax.axis_index("head")


def item_here(z, g):
    r = (z - 2 * (g // 2) + ZC) % ZC
    return r % 4 != 0, 6 * (g // 2) + r % 4 - 1 + 3 * (r // 4), g % 2


def item_z(head):
    k = head % 6
    return (k % 3 + 1 + 4 * (k // 3) + 2 * (head // 6)) % ZC


def greet(z, w, g):
    barrier = pltpu.get_barrier_semaphore()

    def hello(i, carry):
        zz, gg = i // PARTS, i % PARTS

        @pl.when(jnp.logical_or(zz != z, gg != g))
        def _():
            pl.semaphore_signal(barrier, inc=1, device_id=(zz * WC + w, gg), device_id_type=MESH)

        return carry

    lax.fori_loop(0, ZC * PARTS, hello, 0)

    @pl.when(w > 0)
    def _():
        pl.semaphore_signal(barrier, inc=1, device_id=(z * WC + w - 1, g), device_id_type=MESH)

    @pl.when(w < WC - 1)
    def _():
        pl.semaphore_signal(barrier, inc=1, device_id=(z * WC + w + 1, g), device_id_type=MESH)

    return barrier


def met(barrier, w):
    beside = jnp.where(jnp.logical_or(w == 0, w == WC - 1), 1, 2)
    pl.semaphore_wait(barrier, ZC * PARTS - 1 + beside)


def remote(src, dst, send_sem, recv_sem, tile, head):
    return pltpu.make_async_remote_copy(
        src_ref=src, dst_ref=dst, send_sem=send_sem, recv_sem=recv_sem, device_id=(tile, head), device_id_type=MESH
    )


def send(src, dst, send_sem, recv_sem, tile, head, own):
    @pl.when(own)
    def _():
        pltpu.make_async_copy(src, dst, recv_sem).start()

    @pl.when(jnp.logical_not(own))
    def _():
        remote(src, dst, send_sem, recv_sem, tile, head).start()


def sent(src, dst, send_sem, recv_sem, tile, head, own):
    @pl.when(jnp.logical_not(own))
    def _():
        remote(src, dst, send_sem, recv_sem, tile, head).wait_send()


def spread_kernel(
    q_ref, k_ref, v_ref, o_ref, g_ref, mask_ref,
    kv_ref, qg_ref, small_ref,
    given, kv_out, qg_out, small_out,
    given_sem, kv_sent, qg_sent, small_sent, kv_sem, qg_sem, small_sem, side_sent, side_sem, core_sent, core_sem,
):
    z, w, g = place()
    loads = [pltpu.make_async_copy(ref, given.at[i], given_sem.at[i]) for i, ref in enumerate((k_ref, v_ref, q_ref, g_ref, o_ref))]
    for load in loads:
        load.start()
    barrier = greet(z, w, g)
    busy, head, half = item_here(z, g)
    t, h = z // 4, z % 4
    to_half, qslot = h // 2, z // 4 * 2 + h % 2
    slot = t * 3 + h - to_half
    source = g * 4 + qslot
    base = 3 * source // 4

    for i, load in enumerate(loads[:2]):
        load.wait()
        for j in range(HEADS):
            kv_out[j, i] = given[i, :, j * HDIM : (j + 1) * HDIM]

    met(barrier, w)

    def target(s):
        j = (base + s) % HEADS
        zj, gj = item_z(j), 2 * (j // 6) + to_half
        return j, zj * WC + w, gj, jnp.logical_and(zj == z, gj == g)

    def kv_copy(s):
        j, tile, gj, own = target(s)
        return kv_out.at[j], kv_ref.at[1, slot, g], kv_sent.at[j], kv_sem.at[qslot * PARTS + g], tile, gj, own

    def qg_copy(s):
        j, tile, gj, own = target(s)
        return qg_out.at[j], qg_ref.at[qslot, g], qg_sent.at[j], qg_sem.at[qslot * PARTS + g], tile, gj, own

    def small_copy(s):
        j, tile, gj, own = target(s)
        return small_out.at[j], small_ref.at[qslot, g], small_sent.at[j], small_sem.at[qslot * PARTS + g], tile, gj, own

    def start_kv(s, carry):
        send(*kv_copy(s))
        return carry

    lax.fori_loop(0, HEADS, start_kv, 0)

    kept = mask_ref[...].astype(F32)
    kept = jnp.concatenate([kept, jnp.zeros((1, HDIM - kept.shape[1]), F32)], axis=1)
    for load in loads[2:]:
        load.wait()
    for j in range(HEADS):
        cols = slice(j * HDIM, (j + 1) * HDIM)
        qg_out[j, 0] = given[2, :, cols]
        grad = given[3, :, cols]
        qg_out[j, 1] = grad
        prod = grad.astype(F32) * given[4, :, cols].astype(F32)
        prod = jnp.concatenate([prod, jnp.zeros((HDIM - PIECE, HDIM), F32)], axis=0)
        delta = jnp.sum(prod.T, axis=0, keepdims=True)
        small_out[j] = jnp.concatenate([delta, kept, jnp.zeros((6, HDIM), F32)], axis=0)

    def start_qg(s, carry):
        send(*qg_copy(s))
        send(*small_copy(s))
        return carry

    lax.fori_loop(0, HEADS, start_qg, 0)

    def to_side(p, c, side):
        row = p // 2 * 3 + p % 2 + half
        i = p * PARTS + c
        return remote(
            kv_ref.at[1, row, c], kv_ref.at[2 - 2 * side, row, c], side_sent.at[side, i], side_sem.at[1 - side, i],
            z * WC + w + 2 * side - 1, g,
        )

    def to_core(p, c, col):
        i = p // 2 * PARTS + c
        return remote(
            kv_ref.at[col, p // 2 * 3 + 1, c], kv_ref.at[col, p // 2 * 3 + 2 * half, c],
            core_sent.at[col, i], core_sem.at[col, i], z * WC + w, g + 1 - 2 * half,
        )

    def here(ref, arrived_sem):
        return pltpu.make_async_copy(ref, ref, arrived_sem)

    def near(side):
        return w > 0 if side == 0 else w < WC - 1

    @pl.when(busy)
    def _():
        first = (4 * head + 3) // 3

        def forward(i, carry):
            lin = (first - i + 16) % 16
            c, p = lin // 4, lin % 4
            here(kv_ref.at[1, p // 2 * 3 + p % 2 + half, c], kv_sem.at[p * PARTS + c]).wait()
            for side in (0, 1):

                @pl.when(near(side))
                def _():
                    to_side(p, c, side).start()

            @pl.when(p % 2 + half == 1)
            def _():
                to_core(p, c, 1).start()

            return carry

        lax.fori_loop(0, 16, forward, 0)

        def side_in(i, carry):
            lin = (first - i + 16) % 16
            c, p = lin // 4, lin % 4
            for side in (0, 1):

                @pl.when(near(side))
                def _():
                    here(kv_ref.at[2 * side, p // 2 * 3 + p % 2 + half, c], side_sem.at[side, p * PARTS + c]).wait()

                    @pl.when(p % 2 + half == 1)
                    def _():
                        to_core(p, c, 2 * side).start()

            return carry

        lax.fori_loop(0, 16, side_in, 0)

        def arrive(i, carry):
            p, c = i // PARTS, i % PARTS
            here(qg_ref.at[p, c], qg_sem.at[i]).wait()
            here(small_ref.at[p, c], small_sem.at[i]).wait()
            for side in (0, 1):

                @pl.when(near(side))
                def _():
                    to_side(p, c, side).wait_send()

            return carry

        lax.fori_loop(0, 16, arrive, 0)

        def core_in(i, carry):
            p, c = i // PARTS * 2, i % PARTS

            def both(col):
                here(kv_ref.at[col, i // PARTS * 3 + 2 * (1 - half), c], core_sem.at[col, i]).wait()
                to_core(p, c, col).wait_send()

            both(1)
            for side in (0, 1):

                @pl.when(near(side))
                def _():
                    both(2 * side)

            return carry

        lax.fori_loop(0, 2 * PARTS, core_in, 0)

    def finish(s, carry):
        sent(*kv_copy(s))
        sent(*qg_copy(s))
        sent(*small_copy(s))
        return carry

    lax.fori_loop(0, HEADS, finish, 0)


def spread(q, k, v, o, g, mask):
    vmem = pl.BlockSpec(memory_space=pltpu.VMEM)
    hbm = pl.BlockSpec(memory_space=pl.ANY)
    sem = pltpu.SemaphoreType.DMA
    return pl.pallas_call(
        spread_kernel,
        out_shape=(
            jax.ShapeDtypeStruct((3, 6, PARTS, 2, PIECE, HDIM), BF16),
            jax.ShapeDtypeStruct((4, PARTS, 2, PIECE, HDIM), BF16),
            jax.ShapeDtypeStruct((4, PARTS, 8, HDIM), F32),
        ),
        in_specs=[hbm] * 5 + [vmem],
        out_specs=(hbm, hbm, hbm),
        scratch_shapes=[
            pltpu.VMEM((5, PIECE, HEADS * HDIM), BF16),
            pltpu.VMEM((HEADS, 2, PIECE, HDIM), BF16),
            pltpu.VMEM((HEADS, 2, PIECE, HDIM), BF16),
            pltpu.VMEM((HEADS, 8, HDIM), F32),
            sem((5,)),
            sem((HEADS,)),
            sem((HEADS,)),
            sem((HEADS,)),
            sem((16,)),
            sem((16,)),
            sem((16,)),
            sem((2, 16)),
            sem((2, 16)),
            sem((3, 2 * PARTS)),
            sem((3, 2 * PARTS)),
        ],
        compiler_params=pltpu.CompilerParams(
            collective_id=0, has_side_effects=True, vmem_limit_bytes=60 * 1024 * 1024
        ),
    )(q, k, v, o, g, mask)


def dot(a, b, dims):
    return lax.dot_general(a, b, (dims, ((), ())), preferred_element_type=F32)


def attend_kernel(
    kv_any, qg_any, small_any,
    own_ref, halo_ref, outer_ref, inner_ref,
    kv_ref, qg_ref, small_ref, mask_ref, load_sem, weights, top, total, alpha, query_t, terms, active, queries_t, grads_t,
):
    z, w, g = place()
    busy, _, half = item_here(z, g)

    @pl.when(busy)
    def _():
        loads = [
            pltpu.make_async_copy(kv_any, kv_ref, load_sem.at[0]),
            pltpu.make_async_copy(qg_any, qg_ref, load_sem.at[1]),
            pltpu.make_async_copy(small_any, small_ref, load_sem.at[2]),
            pltpu.make_async_copy(small_any.at[:, 0], mask_ref, load_sem.at[3]),
        ]
        for load in loads:
            load.start()
        terms[...] = jnp.zeros(terms.shape, F32)
        for load in loads:
            load.wait()

        def query(q, carry):
            t, row = q // 2, q % 2 + half
            queries = qg_ref[q, :, 0].reshape(TILE, HDIM)
            grads = qg_ref[q, :, 1].reshape(TILE, HDIM)
            delta = jnp.concatenate([small_ref[q, c, 0:1, :PIECE] for c in range(PARTS)], axis=1)
            query_t[...] = jnp.zeros((HDIM, TILE), F32)
            centre = 6 + 3 * t + row
            active[0] = centre

            def pick(n, count):
                col, time2, row2 = n // 6, n % 6 // 3, n % 3
                up = row2 - row
                entry = (time2 - t + 1) * 9 + jnp.clip(up + 1, 0, 2) * 3 + col
                near = jnp.logical_and(up >= -1, up <= 1)
                there = jnp.logical_and(w + col >= 1, w + col <= WC)
                kept = jnp.logical_and(jnp.logical_and(near, there), mask_ref[q, 1, entry] > 0.5)
                active[count] = n
                return count + jnp.where(jnp.logical_and(kept, n != centre), 1, 0)

            count = lax.fori_loop(0, 18, pick, 1)

            def keys_of(n):
                return kv_ref[n // 6, n % 6, :, 0].reshape(TILE, HDIM)

            def score(n):
                return dot(keys_of(n), queries, ((1,), (1,))) * (SCALE * LOG2E)

            top[...] = jnp.max(score(centre), axis=0, keepdims=True)
            total[...] = jnp.zeros((8, TILE), F32)

            queries_t[...] = queries.T
            grads_t[...] = grads.T

            def scores(ns):
                keys = jnp.concatenate([keys_of(n) for n in ns], axis=0)
                e = jnp.exp2(dot(keys, queries_t[...], ((1,), (0,))) * (SCALE * LOG2E) - top[...])
                for m, n in enumerate(ns):
                    weights[n] = e[m * TILE : (m + 1) * TILE]
                total[...] += jnp.sum(e.reshape(-1, 8, TILE), axis=0)

            def in_groups(step):
                done = 0
                for size in GROUPS:

                    def some(i, carry, size=size, done=done):
                        step([active[done + size * i + m] for m in range(size)])
                        return carry

                    rounds = (count - done) // size
                    lax.fori_loop(0, rounds, some, 0)
                    done = done + rounds * size

            in_groups(scores)

            @pl.when(jnp.logical_not(jnp.max(total[...]) < 2.0**100))
            def _():
                def higher(i, carry):
                    top[...] = jnp.maximum(top[...], jnp.max(score(active[i]), axis=0, keepdims=True))
                    return carry

                def again(i, carry):
                    scores([active[i]])
                    return carry

                lax.fori_loop(0, count, higher, 0)
                total[...] = jnp.zeros((8, TILE), F32)
                lax.fori_loop(0, count, again, 0)

            alpha[...] = 1.0 / jnp.sum(total[...], axis=0, keepdims=True)

            def grad_terms(ns):
                values = jnp.concatenate([kv_ref[n // 6, n % 6, :, 1].reshape(TILE, HDIM) for n in ns], axis=0)
                probs = jnp.concatenate([weights[n] for n in ns], axis=0) * alpha[...]
                prob_grads = dot(values, grads_t[...], ((1,), (0,)))
                score_grads = (probs * (prob_grads - delta)).astype(BF16)
                key_terms = dot(score_grads, queries, ((1,), (0,)))
                value_terms = dot(probs.astype(BF16), grads, ((1,), (0,)))
                for m, n in enumerate(ns):
                    terms[n, 0] += key_terms[m * TILE : (m + 1) * TILE]
                    terms[n, 1] += value_terms[m * TILE : (m + 1) * TILE]
                keys = jnp.concatenate([keys_of(n) for n in ns], axis=0)
                query_t[...] += dot(keys, score_grads, ((0,), (0,)))

            in_groups(grad_terms)
            halo_ref[3, t, :, q % 2] = (query_t[...] * SCALE).astype(BF16).T.reshape(PARTS, PIECE, HDIM)
            return carry

        lax.fori_loop(0, 4, query, 0)

        def finish(t, carry):
            for kind, scale in ((0, SCALE), (1, 1.0)):

                def term(col, row):
                    return (terms[6 * col + 3 * t + row, kind] * scale).reshape(PARTS, PIECE, HDIM)

                for col in range(3):
                    halo_ref[col, t, :, kind] = term(col, 2 * (1 - half)).astype(BF16)
                for side in (0, 1):
                    outer_ref[side, t, :, kind] = term(2 * side, 2 * half).astype(BF16)
                    inner_ref[side, t, :, kind] = term(2 * side, 1)
                for row in (0, 1):
                    own_ref[2 * t + row, :, kind] = term(1, row + half)
            return carry

        lax.fori_loop(0, 2, finish, 0)


def attend(kv, qg, small):
    vmem = pl.BlockSpec(memory_space=pltpu.VMEM)
    hbm = pl.BlockSpec(memory_space=pl.ANY)
    block = (PARTS, 2, PIECE, HDIM)
    return pl.pallas_call(
        attend_kernel,
        out_shape=(
            jax.ShapeDtypeStruct((4, *block), F32),
            jax.ShapeDtypeStruct((4, 2, *block), BF16),
            jax.ShapeDtypeStruct((2, 2, *block), BF16),
            jax.ShapeDtypeStruct((2, 2, *block), F32),
        ),
        in_specs=[hbm, hbm, hbm],
        out_specs=(vmem,) * 4,
        scratch_shapes=[
            pltpu.VMEM(kv.shape, BF16),
            pltpu.VMEM(qg.shape, BF16),
            pltpu.VMEM(small.shape, F32),
            pltpu.SMEM((4, 8, HDIM), F32),
            pltpu.SemaphoreType.DMA((4,)),
            pltpu.VMEM((18, TILE, TILE), F32),
            pltpu.VMEM((1, TILE), F32),
            pltpu.VMEM((8, TILE), F32),
            pltpu.VMEM((1, TILE), F32),
            pltpu.VMEM((HDIM, TILE), F32),
            pltpu.VMEM((18, 2, TILE, HDIM), F32),
            pltpu.SMEM((18,), jnp.int32),
            pltpu.VMEM((HDIM, TILE), BF16),
            pltpu.VMEM((HDIM, TILE), BF16),
        ],
        compiler_params=pltpu.CompilerParams(vmem_limit_bytes=60 * 1024 * 1024),
        cost_estimate=pl.CostEstimate(flops=12_000_000_000, bytes_accessed=10_000_000, transcendentals=9_000_000),
    )(kv, qg, small)


def collect_kernel(
    own_any, halo_ref, outer_ref, inner_any,
    oq_ref, ok_ref, ov_ref,
    own_ref, inner_ref, from_core, mixed, beside, ready, got_q, got_kv,
    load_sem, core_sent, core_sem, side_sent, side_sem, q_sent, q_sem, kv_sent, kv_sem,
):
    z, w, g = place()
    loads = [
        pltpu.make_async_copy(inner_any, inner_ref, load_sem.at[0]),
        pltpu.make_async_copy(own_any, own_ref, load_sem.at[1]),
    ]
    for load in loads:
        load.start()
    barrier = greet(z, w, g)
    busy, head, half = item_here(z, g)

    @pl.when(w == 0)
    def _():
        beside[0] = jnp.zeros(beside.shape[1:], BF16)

    @pl.when(w == WC - 1)
    def _():
        beside[1] = jnp.zeros(beside.shape[1:], BF16)

    met(barrier, w)

    def near(side):
        return w > 0 if side == 0 else w < WC - 1

    def here(ref, arrived_sem):
        return pltpu.make_async_copy(ref, ref, arrived_sem)

    def to_core(t, col):
        return remote(
            halo_ref.at[col, t], from_core.at[col, t], core_sent.at[col, t], core_sem.at[col, t],
            z * WC + w, g + 1 - 2 * half,
        )

    def to_side(t, inner, side):
        p = 2 * t + (1 - half if inner else half)
        src = mixed.at[side, t] if inner else outer_ref.at[side, t]
        return remote(
            src, beside.at[1 - side, p], side_sent.at[side, p], side_sem.at[1 - side, p], z * WC + w + 2 * side - 1, g
        )

    def q_copy(i):
        n = (i + 4 * z) % (4 * PARTS)
        q, c = n // PARTS, n % PARTS
        to = q // 2 * 4 + 2 * half + q % 2
        own = jnp.logical_and(to == z, c == g)
        return halo_ref.at[3, q // 2, c, q % 2], got_q.at[head], q_sent.at[n], q_sem.at[head], to * WC + w, c, own

    def kv_copy(p, c):
        to = p // 2 * 4 + p % 2 + 2 * half
        own = jnp.logical_and(to == z, c == g)
        return ready.at[p, c], got_kv.at[head], kv_sent.at[p * PARTS + c], kv_sem.at[head], to * WC + w, c, own

    @pl.when(busy)
    def _():
        for col in (0, 2, 1):
            for t in (0, 1):

                @pl.when(near(col // 2) if col != 1 else w >= 0)
                def _():
                    to_core(t, col).start()

        for t in (0, 1):
            for side in (0, 1):

                @pl.when(near(side))
                def _():
                    to_side(t, False, side).start()

        def start_q(i, carry):
            send(*q_copy(i))
            return carry

        lax.fori_loop(0, 4 * PARTS, start_q, 0)
        for load in loads:
            load.wait()

        for t in (0, 1):
            for side in (0, 1):

                @pl.when(near(side))
                def _():
                    here(from_core.at[2 * side, t], core_sem.at[2 * side, t]).wait()
                    for c in range(PARTS):
                        both = inner_ref[side, t, c] + from_core[2 * side, t, c].astype(F32)
                        mixed[side, t, c] = both.astype(BF16)
                    to_side(t, True, side).start()

        for t in (0, 1):
            here(from_core.at[1, t], core_sem.at[1, t]).wait()
            p = 2 * t + 1 - half
            for c in range(PARTS):
                own_ref[p, c] = own_ref[p, c] + from_core[1, t, c].astype(F32)

        for inner in (False, True):

            def add(i, carry):
                t = (i + z // 4) % 2
                p = 2 * t + (1 - half if inner else half)
                for side in (0, 1):

                    @pl.when(near(side))
                    def _():
                        here(beside.at[side, p], side_sem.at[side, p]).wait()

                for c in range(PARTS):
                    both = own_ref[p, c] + beside[0, p, c].astype(F32) + beside[1, p, c].astype(F32)
                    ready[p, c] = both.astype(BF16)
                    send(*kv_copy(p, c))
                return carry

            lax.fori_loop(0, 2, add, 0)

        for t in (0, 1):
            to_core(t, 1).wait_send()
            for side in (0, 1):

                @pl.when(near(side))
                def _():
                    to_core(t, 2 * side).wait_send()
                    to_side(t, False, side).wait_send()
                    to_side(t, True, side).wait_send()

        def finish(n, carry):
            sent(*kv_copy(n // PARTS, n % PARTS))
            sent(*q_copy(n))
            return carry

        lax.fori_loop(0, 4 * PARTS, finish, 0)

    @pl.when(jnp.logical_not(busy))
    def _():
        for load in loads:
            load.wait()

    for j in range(HEADS):
        cols = slice(j * HDIM, (j + 1) * HDIM)
        here(got_q.at[j], q_sem.at[j]).wait()
        oq_ref[:, cols] = got_q[j]
        here(got_kv.at[j], kv_sem.at[j]).wait()
        ok_ref[:, cols] = got_kv[j, 0]
        ov_ref[:, cols] = got_kv[j, 1]


def collect(own, halo, outer, inner):
    vmem = pl.BlockSpec(memory_space=pltpu.VMEM)
    hbm = pl.BlockSpec(memory_space=pl.ANY)
    sem = pltpu.SemaphoreType.DMA
    out = jax.ShapeDtypeStruct((PIECE, HEADS * HDIM), BF16)
    block = (PARTS, 2, PIECE, HDIM)
    return pl.pallas_call(
        collect_kernel,
        out_shape=(out, out, out),
        in_specs=[hbm] * 4,
        out_specs=(vmem, vmem, vmem),
        scratch_shapes=[
            pltpu.VMEM((4, *block), F32),
            pltpu.VMEM((2, 2, *block), F32),
            pltpu.VMEM((3, 2, *block), BF16),
            pltpu.VMEM((2, 2, *block), BF16),
            pltpu.VMEM((2, 4, *block), BF16),
            pltpu.VMEM((4, *block), BF16),
            pltpu.VMEM((HEADS, PIECE, HDIM), BF16),
            pltpu.VMEM((HEADS, 2, PIECE, HDIM), BF16),
            sem((2,)),
            sem((3, 2)),
            sem((3, 2)),
            sem((2, 4)),
            sem((2, 4)),
            sem((4 * PARTS,)),
            sem((HEADS,)),
            sem((4 * PARTS,)),
            sem((HEADS,)),
        ],
        compiler_params=pltpu.CompilerParams(
            collective_id=1, has_side_effects=True, vmem_limit_bytes=54016 * 1024
        ),
    )(own, halo, outer, inner)


def shards(query_vecs, key_vecs, value_vecs, outputs, out_grads, keep_mask):
    kv, qg, small = spread(query_vecs, key_vecs, value_vecs, outputs, out_grads, keep_mask)
    return collect(*attend(kv, qg, small))


def solution(mesh):
    rows = P(("tile", "head"), None)
    return jax.shard_map(
        shards,
        mesh=mesh,
        in_specs=(rows, rows, rows, rows, rows, P("tile", None)),
        out_specs=(rows, rows, rows),
        check_vma=False,
    )
```

```python
import jax
import jax.numpy as jnp
from jax import lax
from jax.experimental import pallas as pl
from jax.experimental.pallas import tpu as pltpu
from jax.sharding import PartitionSpec as P

MESH = pl.DeviceIdType.MESH
HEADS = 12
HDIM = 128
PIECE = 96
PARTS = 4
TILE = PIECE * PARTS
ROWS = 2 * PIECE + 16
WC = 8
GROUPS = (4, 3, 2, 1)
ZC = 8
SCALE = HDIM**-0.5
LOG2E = 1.4426950408889634
F32 = jnp.float32
BF16 = jnp.bfloat16


def place():
    tile = lax.axis_index("tile")
    return tile // WC, tile % WC, lax.axis_index("head")


def item_here(z, g):
    r = (z - 2 * (g // 2) + ZC) % ZC
    return r % 4 != 0, 6 * (g // 2) + r % 4 - 1 + 3 * (r // 4), g % 2


def item_z(head):
    k = head % 6
    return (k % 3 + 1 + 4 * (k // 3) + 2 * (head // 6)) % ZC


def greet(z, w, g):
    barrier = pltpu.get_barrier_semaphore()

    def hello(i, carry):
        zz, gg = i // PARTS, i % PARTS

        @pl.when(jnp.logical_or(zz != z, gg != g))
        def _():
            pl.semaphore_signal(barrier, inc=1, device_id=(zz * WC + w, gg), device_id_type=MESH)

        return carry

    lax.fori_loop(0, ZC * PARTS, hello, 0)

    @pl.when(w > 0)
    def _():
        pl.semaphore_signal(barrier, inc=1, device_id=(z * WC + w - 1, g), device_id_type=MESH)

    @pl.when(w < WC - 1)
    def _():
        pl.semaphore_signal(barrier, inc=1, device_id=(z * WC + w + 1, g), device_id_type=MESH)

    return barrier


def met(barrier, w):
    beside = jnp.where(jnp.logical_or(w == 0, w == WC - 1), 1, 2)
    pl.semaphore_wait(barrier, ZC * PARTS - 1 + beside)


def remote(src, dst, send_sem, recv_sem, tile, head):
    return pltpu.make_async_remote_copy(
        src_ref=src, dst_ref=dst, send_sem=send_sem, recv_sem=recv_sem, device_id=(tile, head), device_id_type=MESH
    )


def send(src, dst, send_sem, recv_sem, tile, head, own):
    @pl.when(own)
    def _():
        pltpu.make_async_copy(src, dst, recv_sem).start()

    @pl.when(jnp.logical_not(own))
    def _():
        remote(src, dst, send_sem, recv_sem, tile, head).start()


def sent(src, dst, send_sem, recv_sem, tile, head, own):
    @pl.when(jnp.logical_not(own))
    def _():
        remote(src, dst, send_sem, recv_sem, tile, head).wait_send()


def spread_kernel(
    q_ref, k_ref, v_ref, o_ref, g_ref, mask_ref,
    kv_ref, qg_ref,
    given, kv_out, qg_out,
    given_sem, kv_sent, qg_sent, kv_sem, qg_sem, side_sent, side_sem, core_sent, core_sem,
):
    z, w, g = place()
    loads = [pltpu.make_async_copy(ref, given.at[i], given_sem.at[i]) for i, ref in enumerate((k_ref, v_ref, q_ref, g_ref, o_ref))]
    for load in loads:
        load.start()
    barrier = greet(z, w, g)
    busy, head, half = item_here(z, g)
    t, h = z // 4, z % 4
    to_half, qslot = h // 2, z // 4 * 2 + h % 2
    slot = t * 3 + h - to_half
    source = g * 4 + qslot
    base = 3 * source // 4

    for i, load in enumerate(loads[:2]):
        load.wait()
        for j in range(HEADS):
            kv_out[j, i] = given[i, :, j * HDIM : (j + 1) * HDIM]

    met(barrier, w)

    def target(s):
        j = (base + s) % HEADS
        zj, gj = item_z(j), 2 * (j // 6) + to_half
        return j, zj * WC + w, gj, jnp.logical_and(zj == z, gj == g)

    def kv_copy(s):
        j, tile, gj, own = target(s)
        return kv_out.at[j], kv_ref.at[1, slot, g], kv_sent.at[j], kv_sem.at[qslot * PARTS + g], tile, gj, own

    def qg_copy(s):
        j, tile, gj, own = target(s)
        return qg_out.at[j], qg_ref.at[qslot, g], qg_sent.at[j], qg_sem.at[qslot * PARTS + g], tile, gj, own

    def start_kv(s, carry):
        send(*kv_copy(s))
        return carry

    lax.fori_loop(0, HEADS, start_kv, 0)

    kept = mask_ref[...].astype(F32)
    kept = jnp.concatenate([kept, jnp.zeros((1, HDIM - kept.shape[1]), F32)], axis=1)
    for load in loads[2:]:
        load.wait()
    for j in range(HEADS):
        cols = slice(j * HDIM, (j + 1) * HDIM)
        grad = given[3, :, cols]
        prod = grad.astype(F32) * given[4, :, cols].astype(F32)
        prod = jnp.concatenate([prod, jnp.zeros((HDIM - PIECE, HDIM), F32)], axis=0)
        delta = jnp.sum(prod.T, axis=0, keepdims=True)
        high = delta.astype(BF16).astype(F32)
        middle = (delta - high).astype(BF16).astype(F32)
        low = delta - high - middle
        rest = jnp.concatenate([high, middle, low, kept, jnp.zeros((12, HDIM), F32)], axis=0)
        qg_out[j, :PIECE] = given[2, :, cols]
        qg_out[j, PIECE : 2 * PIECE] = grad
        qg_out[j, 2 * PIECE :] = rest.astype(BF16)

    def start_qg(s, carry):
        send(*qg_copy(s))
        return carry

    lax.fori_loop(0, HEADS, start_qg, 0)

    def to_side(p, c, side):
        row = p // 2 * 3 + p % 2 + half
        i = p * PARTS + c
        return remote(
            kv_ref.at[1, row, c], kv_ref.at[2 - 2 * side, row, c], side_sent.at[side, i], side_sem.at[1 - side, i],
            z * WC + w + 2 * side - 1, g,
        )

    def to_core(p, c, col):
        i = p // 2 * PARTS + c
        return remote(
            kv_ref.at[col, p // 2 * 3 + 1, c], kv_ref.at[col, p // 2 * 3 + 2 * half, c],
            core_sent.at[col, i], core_sem.at[col, i], z * WC + w, g + 1 - 2 * half,
        )

    def here(ref, arrived_sem):
        return pltpu.make_async_copy(ref, ref, arrived_sem)

    def near(side):
        return w > 0 if side == 0 else w < WC - 1

    @pl.when(busy)
    def _():
        first = (4 * head + 3) // 3

        def forward(i, carry):
            lin = (first - i + 16) % 16
            c, p = lin // 4, lin % 4
            here(kv_ref.at[1, p // 2 * 3 + p % 2 + half, c], kv_sem.at[p * PARTS + c]).wait()
            for side in (0, 1):

                @pl.when(near(side))
                def _():
                    to_side(p, c, side).start()

            @pl.when(p % 2 + half == 1)
            def _():
                to_core(p, c, 1).start()

            return carry

        lax.fori_loop(0, 16, forward, 0)

        def side_in(i, carry):
            lin = (first - i + 16) % 16
            c, p = lin // 4, lin % 4
            for side in (0, 1):

                @pl.when(near(side))
                def _():
                    here(kv_ref.at[2 * side, p // 2 * 3 + p % 2 + half, c], side_sem.at[side, p * PARTS + c]).wait()

                    @pl.when(p % 2 + half == 1)
                    def _():
                        to_core(p, c, 2 * side).start()

            return carry

        lax.fori_loop(0, 16, side_in, 0)

        def arrive(i, carry):
            p, c = i // PARTS, i % PARTS
            here(qg_ref.at[p, c], qg_sem.at[i]).wait()
            for side in (0, 1):

                @pl.when(near(side))
                def _():
                    to_side(p, c, side).wait_send()

            return carry

        lax.fori_loop(0, 16, arrive, 0)

        def core_in(i, carry):
            p, c = i // PARTS * 2, i % PARTS

            def both(col):
                here(kv_ref.at[col, i // PARTS * 3 + 2 * (1 - half), c], core_sem.at[col, i]).wait()
                to_core(p, c, col).wait_send()

            both(1)
            for side in (0, 1):

                @pl.when(near(side))
                def _():
                    both(2 * side)

            return carry

        lax.fori_loop(0, 2 * PARTS, core_in, 0)

    def finish(s, carry):
        sent(*kv_copy(s))
        sent(*qg_copy(s))
        return carry

    lax.fori_loop(0, HEADS, finish, 0)


def spread(q, k, v, o, g, mask):
    vmem = pl.BlockSpec(memory_space=pltpu.VMEM)
    hbm = pl.BlockSpec(memory_space=pl.ANY)
    sem = pltpu.SemaphoreType.DMA
    return pl.pallas_call(
        spread_kernel,
        out_shape=(
            jax.ShapeDtypeStruct((3, 6, PARTS, 2, PIECE, HDIM), BF16),
            jax.ShapeDtypeStruct((4, PARTS, ROWS, HDIM), BF16),
        ),
        in_specs=[hbm] * 5 + [vmem],
        out_specs=(hbm, hbm),
        scratch_shapes=[
            pltpu.VMEM((5, PIECE, HEADS * HDIM), BF16),
            pltpu.VMEM((HEADS, 2, PIECE, HDIM), BF16),
            pltpu.VMEM((HEADS, ROWS, HDIM), BF16),
            sem((5,)),
            sem((HEADS,)),
            sem((HEADS,)),
            sem((16,)),
            sem((16,)),
            sem((2, 16)),
            sem((2, 16)),
            sem((3, 2 * PARTS)),
            sem((3, 2 * PARTS)),
        ],
        compiler_params=pltpu.CompilerParams(
            collective_id=0, has_side_effects=True, vmem_limit_bytes=60 * 1024 * 1024
        ),
    )(q, k, v, o, g, mask)


def dot(a, b, dims):
    return lax.dot_general(a, b, (dims, ((), ())), preferred_element_type=F32)


def attend_kernel(
    kv_any, qg_any,
    own_ref, halo_ref, outer_ref, inner_ref,
    kv_ref, qg_ref, load_sem, weights, top, total, alpha, query_t, terms, active, counts, queries_t, grads_t,
):
    z, w, g = place()
    busy, _, half = item_here(z, g)

    @pl.when(busy)
    def _():
        loads = [
            pltpu.make_async_copy(qg_any, qg_ref, load_sem.at[0]),
            pltpu.make_async_copy(kv_any.at[1], kv_ref.at[1], load_sem.at[1]),
            pltpu.make_async_copy(kv_any.at[0], kv_ref.at[0], load_sem.at[2]),
            pltpu.make_async_copy(kv_any.at[2], kv_ref.at[2], load_sem.at[3]),
        ]
        for load in loads:
            load.start()
        terms[...] = jnp.zeros(terms.shape, F32)
        for load in loads[:2]:
            load.wait()

        for q in range(4):
            t = q // 2
            flags = qg_ref[q, 0, 2 * PIECE :].astype(F32)[3:4]
            bit = lax.broadcasted_iota(jnp.int32, (1, HDIM), 1) - 9 * (1 - t)
            inside = jnp.logical_and(bit >= 0, bit < 18)
            power = jnp.where(inside, jnp.left_shift(1, jnp.clip(bit, 0, 17)), 0)
            bits = jnp.sum(power.astype(F32) * flags).astype(jnp.int32)
            count = jnp.int32(0)
            for n in range(18):
                col, time2, row2 = n // 6, n % 6 // 3, n % 3
                for up in (-1, 0, 1):
                    if not 0 <= row2 - up - q % 2 <= 1 or (up == 0 and time2 == t and col == 1):
                        continue
                    entry = time2 * 9 + (up + 1) * 3 + col
                    kept = jnp.logical_and((bits >> entry) % 2 == 1, half == row2 - up - q % 2)
                    if col != 1:
                        kept = jnp.logical_and(kept, w > 0 if col == 0 else w < WC - 1)
                    active[q, count] = n
                    count = count + jnp.where(kept, 1, 0)
            counts[q] = count

        def query(q, carry):
            t, row = q // 2, q % 2 + half
            queries = qg_ref[q, :, :PIECE].reshape(TILE, HDIM)
            grads = qg_ref[q, :, PIECE : 2 * PIECE].reshape(TILE, HDIM)
            rest = qg_ref[q, :, 2 * PIECE :].astype(F32)
            deltas = rest[:, 0:1, :PIECE] + rest[:, 1:2, :PIECE] + rest[:, 2:3, :PIECE]
            delta = jnp.concatenate([deltas[c] for c in range(PARTS)], axis=1)
            query_t[...] = jnp.zeros((HDIM, TILE), F32)
            centre = 6 + 3 * t + row
            count = counts[q]

            def keys_of(n):
                return kv_ref[n // 6, n % 6, :, 0].reshape(TILE, HDIM)

            queries_t[...] = queries.T

            def score(n):
                return dot(keys_of(n), queries_t[...], ((1,), (0,))) * (SCALE * LOG2E)

            own = score(centre)
            first = jnp.max(own, axis=0, keepdims=True)
            top[...] = first
            own = jnp.exp2(own - first)
            weights[centre] = own
            total[...] = jnp.sum(own.reshape(-1, 8, TILE), axis=0)

            @pl.when(q == 0)
            def _():
                for load in loads[2:]:
                    load.wait()


            grads_t[...] = grads.T

            def scores(ns):
                keys = jnp.concatenate([keys_of(n) for n in ns], axis=0)
                e = jnp.exp2(dot(keys, queries_t[...], ((1,), (0,))) * (SCALE * LOG2E) - top[...])
                for m, n in enumerate(ns):
                    weights[n] = e[m * TILE : (m + 1) * TILE]
                total[...] += jnp.sum(e.reshape(-1, 8, TILE), axis=0)

            def in_groups(step):
                done = 0
                for size in GROUPS:

                    def some(i, carry, size=size, done=done):
                        step([active[q, done + size * i + m] for m in range(size)])
                        return carry

                    rounds = (count - done) // size
                    lax.fori_loop(0, rounds, some, 0)
                    done = done + rounds * size

            in_groups(scores)

            @pl.when(jnp.logical_not(jnp.max(total[...]) < 2.0**100))
            def _():
                def higher(i, carry):
                    top[...] = jnp.maximum(top[...], jnp.max(score(active[q, i]), axis=0, keepdims=True))
                    return carry

                def again(i, carry):
                    scores([active[q, i]])
                    return carry

                lax.fori_loop(0, count, higher, 0)
                total[...] = jnp.zeros((8, TILE), F32)
                scores([centre])
                lax.fori_loop(0, count, again, 0)

            alpha[...] = 1.0 / jnp.sum(total[...], axis=0, keepdims=True)

            def grad_terms(ns):
                values = jnp.concatenate([kv_ref[n // 6, n % 6, :, 1].reshape(TILE, HDIM) for n in ns], axis=0)
                probs = jnp.concatenate([weights[n] for n in ns], axis=0) * alpha[...]
                prob_grads = dot(values, grads_t[...], ((1,), (0,)))
                score_grads = (probs * (prob_grads - delta)).astype(BF16)
                key_terms = dot(score_grads, queries, ((1,), (0,)))
                value_terms = dot(probs.astype(BF16), grads, ((1,), (0,)))
                for m, n in enumerate(ns):
                    terms[n, 0] += key_terms[m * TILE : (m + 1) * TILE]
                    terms[n, 1] += value_terms[m * TILE : (m + 1) * TILE]
                keys = jnp.concatenate([keys_of(n) for n in ns], axis=0)
                query_t[...] += dot(keys, score_grads, ((0,), (0,)))

            grad_terms([centre])
            in_groups(grad_terms)
            halo_ref[3, t, :, q % 2] = (query_t[...] * SCALE).astype(BF16).T.reshape(PARTS, PIECE, HDIM)
            return carry

        lax.fori_loop(0, 4, query, 0)

        def finish(t, carry):
            for kind, scale in ((0, SCALE), (1, 1.0)):

                def term(col, row):
                    return (terms[6 * col + 3 * t + row, kind] * scale).reshape(PARTS, PIECE, HDIM)

                for col in range(3):
                    halo_ref[col, t, :, kind] = term(col, 2 * (1 - half)).astype(BF16)
                for side in (0, 1):
                    outer_ref[side, t, :, kind] = term(2 * side, 2 * half).astype(BF16)
                    inner_ref[side, t, :, kind] = term(2 * side, 1)
                for row in (0, 1):
                    own_ref[2 * t + row, :, kind] = term(1, row + half)
            return carry

        lax.fori_loop(0, 2, finish, 0)


def attend(kv, qg):
    vmem = pl.BlockSpec(memory_space=pltpu.VMEM)
    hbm = pl.BlockSpec(memory_space=pl.ANY)
    block = (PARTS, 2, PIECE, HDIM)
    return pl.pallas_call(
        attend_kernel,
        out_shape=(
            jax.ShapeDtypeStruct((4, *block), F32),
            jax.ShapeDtypeStruct((4, 2, *block), BF16),
            jax.ShapeDtypeStruct((2, 2, *block), BF16),
            jax.ShapeDtypeStruct((2, 2, *block), F32),
        ),
        in_specs=[hbm, hbm],
        out_specs=(vmem,) * 4,
        scratch_shapes=[
            pltpu.VMEM(kv.shape, BF16),
            pltpu.VMEM(qg.shape, BF16),
            pltpu.SemaphoreType.DMA((4,)),
            pltpu.VMEM((18, TILE, TILE), F32),
            pltpu.VMEM((1, TILE), F32),
            pltpu.VMEM((8, TILE), F32),
            pltpu.VMEM((1, TILE), F32),
            pltpu.VMEM((HDIM, TILE), F32),
            pltpu.VMEM((18, 2, TILE, HDIM), F32),
            pltpu.SMEM((4, 19), jnp.int32),
            pltpu.SMEM((4,), jnp.int32),
            pltpu.VMEM((HDIM, TILE), BF16),
            pltpu.VMEM((HDIM, TILE), BF16),
        ],
        compiler_params=pltpu.CompilerParams(vmem_limit_bytes=60 * 1024 * 1024),
        cost_estimate=pl.CostEstimate(flops=12_000_000_000, bytes_accessed=10_000_000, transcendentals=9_000_000),
    )(kv, qg)


def collect_kernel(
    own_any, halo_ref, outer_ref, inner_any,
    oq_ref, ok_ref, ov_ref,
    own_ref, inner_ref, from_core, mixed, beside, ready, got_q, got_kv,
    load_sem, core_sent, core_sem, side_sent, side_sem, q_sent, q_sem, kv_sent, kv_sem,
):
    z, w, g = place()
    loads = [
        pltpu.make_async_copy(inner_any, inner_ref, load_sem.at[0]),
        pltpu.make_async_copy(own_any, own_ref, load_sem.at[1]),
    ]
    for load in loads:
        load.start()
    barrier = greet(z, w, g)
    busy, head, half = item_here(z, g)

    @pl.when(w == 0)
    def _():
        beside[0] = jnp.zeros(beside.shape[1:], BF16)

    @pl.when(w == WC - 1)
    def _():
        beside[1] = jnp.zeros(beside.shape[1:], BF16)

    met(barrier, w)

    def near(side):
        return w > 0 if side == 0 else w < WC - 1

    def here(ref, arrived_sem):
        return pltpu.make_async_copy(ref, ref, arrived_sem)

    def to_core(t, col):
        return remote(
            halo_ref.at[col, t], from_core.at[col, t], core_sent.at[col, t], core_sem.at[col, t],
            z * WC + w, g + 1 - 2 * half,
        )

    def to_side(t, c, inner, side):
        p = 2 * t + (1 - half if inner else half)
        i = p * PARTS + c
        src = mixed.at[side, t, c] if inner else outer_ref.at[side, t, c]
        return remote(
            src, beside.at[1 - side, p, c], side_sent.at[side, i], side_sem.at[1 - side, i],
            z * WC + w + 2 * side - 1, g,
        )

    def q_copy(i):
        n = (i + 4 * z) % (4 * PARTS)
        q, c = n // PARTS, n % PARTS
        to = q // 2 * 4 + 2 * half + q % 2
        own = jnp.logical_and(to == z, c == g)
        return halo_ref.at[3, q // 2, c, q % 2], got_q.at[head], q_sent.at[n], q_sem.at[head], to * WC + w, c, own

    def kv_copy(p, c):
        to = p // 2 * 4 + p % 2 + 2 * half
        own = jnp.logical_and(to == z, c == g)
        return ready.at[p, c], got_kv.at[head], kv_sent.at[p * PARTS + c], kv_sem.at[head], to * WC + w, c, own

    @pl.when(busy)
    def _():
        for col in (0, 2, 1):
            for t in (0, 1):

                @pl.when(near(col // 2) if col != 1 else w >= 0)
                def _():
                    to_core(t, col).start()

        def outer_out(i, carry):
            for side in (0, 1):

                @pl.when(near(side))
                def _():
                    to_side(i % 2, i // 2, False, side).start()

            return carry

        lax.fori_loop(0, 2 * PARTS, outer_out, 0)

        def start_q(i, carry):
            send(*q_copy(i))
            return carry

        lax.fori_loop(0, 4 * PARTS, start_q, 0)

        for load in loads:
            load.wait()

        def add(t, c, inner):
            p = 2 * t + (1 - half if inner else half)
            for side in (0, 1):

                @pl.when(near(side))
                def _():
                    here(beside.at[side, p, c], side_sem.at[side, p * PARTS + c]).wait()

            both = own_ref[p, c] + beside[0, p, c].astype(F32) + beside[1, p, c].astype(F32)
            ready[p, c] = both.astype(BF16)
            send(*kv_copy(p, c))

        for t in (0, 1):
            for side in (0, 1):

                @pl.when(near(side))
                def _():
                    here(from_core.at[2 * side, t], core_sem.at[2 * side, t]).wait()

            def inner_out(c, carry):
                for side in (0, 1):

                    @pl.when(near(side))
                    def _():
                        both = inner_ref[side, t, c] + from_core[2 * side, t, c].astype(F32)
                        mixed[side, t, c] = both.astype(BF16)
                        to_side(t, c, True, side).start()

                return carry

            lax.fori_loop(0, PARTS, inner_out, 0)

        for t in (0, 1):
            here(from_core.at[1, t], core_sem.at[1, t]).wait()
            p = 2 * t + 1 - half
            for c in range(PARTS):
                own_ref[p, c] = own_ref[p, c] + from_core[1, t, c].astype(F32)

        def add_outer(i, carry):
            add(i % 2, i // 2, False)
            return carry

        lax.fori_loop(0, 2 * PARTS, add_outer, 0)

        def add_inner(i, carry):
            add(i // PARTS, i % PARTS, True)
            return carry

        lax.fori_loop(0, 2 * PARTS, add_inner, 0)

        for t in (0, 1):
            to_core(t, 1).wait_send()
            for side in (0, 1):

                @pl.when(near(side))
                def _():
                    to_core(t, 2 * side).wait_send()

        def side_sends(i, carry):
            for side in (0, 1):

                @pl.when(near(side))
                def _():
                    to_side(i % 2, i // 2, False, side).wait_send()
                    to_side(i % 2, i // 2, True, side).wait_send()

            return carry

        lax.fori_loop(0, 2 * PARTS, side_sends, 0)

        def finish(n, carry):
            sent(*kv_copy(n // PARTS, n % PARTS))
            sent(*q_copy(n))
            return carry

        lax.fori_loop(0, 4 * PARTS, finish, 0)

    @pl.when(jnp.logical_not(busy))
    def _():
        for load in loads:
            load.wait()

    for j in range(HEADS):
        cols = slice(j * HDIM, (j + 1) * HDIM)
        here(got_q.at[j], q_sem.at[j]).wait()
        oq_ref[:, cols] = got_q[j]
        here(got_kv.at[j], kv_sem.at[j]).wait()
        ok_ref[:, cols] = got_kv[j, 0]
        ov_ref[:, cols] = got_kv[j, 1]


def collect(own, halo, outer, inner):
    vmem = pl.BlockSpec(memory_space=pltpu.VMEM)
    hbm = pl.BlockSpec(memory_space=pl.ANY)
    sem = pltpu.SemaphoreType.DMA
    out = jax.ShapeDtypeStruct((PIECE, HEADS * HDIM), BF16)
    block = (PARTS, 2, PIECE, HDIM)
    return pl.pallas_call(
        collect_kernel,
        out_shape=(out, out, out),
        in_specs=[hbm] * 4,
        out_specs=(vmem, vmem, vmem),
        scratch_shapes=[
            pltpu.VMEM((4, *block), F32),
            pltpu.VMEM((2, 2, *block), F32),
            pltpu.VMEM((3, 2, *block), BF16),
            pltpu.VMEM((2, 2, *block), BF16),
            pltpu.VMEM((2, 4, *block), BF16),
            pltpu.VMEM((4, *block), BF16),
            pltpu.VMEM((HEADS, PIECE, HDIM), BF16),
            pltpu.VMEM((HEADS, 2, PIECE, HDIM), BF16),
            sem((2,)),
            sem((3, 2)),
            sem((3, 2)),
            sem((2, 16)),
            sem((2, 16)),
            sem((4 * PARTS,)),
            sem((HEADS,)),
            sem((4 * PARTS,)),
            sem((HEADS,)),
        ],
        compiler_params=pltpu.CompilerParams(
            collective_id=1, has_side_effects=True, vmem_limit_bytes=54016 * 1024
        ),
    )(own, halo, outer, inner)


def shards(query_vecs, key_vecs, value_vecs, outputs, out_grads, keep_mask):
    return collect(*attend(*spread(query_vecs, key_vecs, value_vecs, outputs, out_grads, keep_mask)))


def solution(mesh):
    rows = P(("tile", "head"), None)
    return jax.shard_map(
        shards,
        mesh=mesh,
        in_specs=(rows, rows, rows, rows, rows, P("tile", None)),
        out_specs=(rows, rows, rows),
        check_vma=False,
    )
```

```python
import jax
import jax.numpy as jnp
from jax import lax
from jax.experimental import pallas as pl
from jax.experimental.pallas import tpu as pltpu
from jax.sharding import PartitionSpec as P

MESH = pl.DeviceIdType.MESH
HEADS = 12
HDIM = 128
PIECE = 96
PARTS = 4
TILE = PIECE * PARTS
ROWS = 2 * PIECE + 16
WC = 8
GROUPS = (6, 4, 3, 2, 1)
ZC = 8
SCALE = HDIM**-0.5
LOG2E = 1.4426950408889634
F32 = jnp.float32
BF16 = jnp.bfloat16


def place():
    tile = lax.axis_index("tile")
    return tile // WC, tile % WC, lax.axis_index("head")


def item_here(z, g):
    r = (z - 2 * (g // 2) + ZC) % ZC
    return r % 4 != 0, 6 * (g // 2) + r % 4 - 1 + 3 * (r // 4), g % 2


def item_z(head):
    k = head % 6
    return (k % 3 + 1 + 4 * (k // 3) + 2 * (head // 6)) % ZC


def greet(z, w, g):
    barrier = pltpu.get_barrier_semaphore()

    def hello(i, carry):
        zz, gg = i // PARTS, i % PARTS

        @pl.when(jnp.logical_or(zz != z, gg != g))
        def _():
            pl.semaphore_signal(barrier, inc=1, device_id=(zz * WC + w, gg), device_id_type=MESH)

        return carry

    lax.fori_loop(0, ZC * PARTS, hello, 0)

    @pl.when(w > 0)
    def _():
        pl.semaphore_signal(barrier, inc=1, device_id=(z * WC + w - 1, g), device_id_type=MESH)

    @pl.when(w < WC - 1)
    def _():
        pl.semaphore_signal(barrier, inc=1, device_id=(z * WC + w + 1, g), device_id_type=MESH)

    return barrier


def met(barrier, w):
    beside = jnp.where(jnp.logical_or(w == 0, w == WC - 1), 1, 2)
    pl.semaphore_wait(barrier, ZC * PARTS - 1 + beside)


def remote(src, dst, send_sem, recv_sem, tile, head):
    return pltpu.make_async_remote_copy(
        src_ref=src, dst_ref=dst, send_sem=send_sem, recv_sem=recv_sem, device_id=(tile, head), device_id_type=MESH
    )


def send(src, dst, send_sem, recv_sem, tile, head, own):
    @pl.when(own)
    def _():
        pltpu.make_async_copy(src, dst, recv_sem).start()

    @pl.when(jnp.logical_not(own))
    def _():
        remote(src, dst, send_sem, recv_sem, tile, head).start()


def sent(src, dst, send_sem, recv_sem, tile, head, own):
    @pl.when(jnp.logical_not(own))
    def _():
        remote(src, dst, send_sem, recv_sem, tile, head).wait_send()


def spread_kernel(
    q_ref, k_ref, v_ref, o_ref, g_ref, mask_ref,
    kv_ref, qg_ref,
    given, kv_out, qg_out,
    given_sem, kv_sent, qg_sent, kv_sem, qg_sem, side_sent, side_sem, core_sent, core_sem,
):
    z, w, g = place()
    loads = [pltpu.make_async_copy(ref, given.at[i], given_sem.at[i]) for i, ref in enumerate((k_ref, v_ref, q_ref, g_ref, o_ref))]
    for load in loads:
        load.start()
    barrier = greet(z, w, g)
    busy, head, half = item_here(z, g)
    t, h = z // 4, z % 4
    to_half, qslot = h // 2, z // 4 * 2 + h % 2
    slot = t * 3 + h - to_half
    source = g * 4 + qslot
    base = 3 * source // 4

    for i, load in enumerate(loads[:2]):
        load.wait()
        for j in range(HEADS):
            kv_out[j, i] = given[i, :, j * HDIM : (j + 1) * HDIM]

    met(barrier, w)

    def target(s):
        j = (base + s) % HEADS
        zj, gj = item_z(j), 2 * (j // 6) + to_half
        return j, zj * WC + w, gj, jnp.logical_and(zj == z, gj == g)

    def kv_copy(s):
        j, tile, gj, own = target(s)
        return kv_out.at[j], kv_ref.at[1, slot, g], kv_sent.at[j], kv_sem.at[qslot * PARTS + g], tile, gj, own

    def qg_copy(s):
        j, tile, gj, own = target(s)
        return qg_out.at[j], qg_ref.at[qslot, g], qg_sent.at[j], qg_sem.at[qslot * PARTS + g], tile, gj, own

    def start_kv(s, carry):
        send(*kv_copy(s))
        return carry

    lax.fori_loop(0, HEADS, start_kv, 0)

    kept = mask_ref[...].astype(F32)
    kept = jnp.concatenate([kept, jnp.zeros((1, HDIM - kept.shape[1]), F32)], axis=1)
    for load in loads[2:]:
        load.wait()
    for j in range(HEADS):
        cols = slice(j * HDIM, (j + 1) * HDIM)
        grad = given[3, :, cols]
        prod = grad.astype(F32) * given[4, :, cols].astype(F32)
        prod = jnp.concatenate([prod, jnp.zeros((HDIM - PIECE, HDIM), F32)], axis=0)
        delta = jnp.sum(prod.T, axis=0, keepdims=True)
        high = delta.astype(BF16).astype(F32)
        middle = (delta - high).astype(BF16).astype(F32)
        low = delta - high - middle
        rest = jnp.concatenate([high, middle, low, kept, jnp.zeros((12, HDIM), F32)], axis=0)
        qg_out[j, :PIECE] = given[2, :, cols]
        qg_out[j, PIECE : 2 * PIECE] = grad
        qg_out[j, 2 * PIECE :] = rest.astype(BF16)

    def start_qg(s, carry):
        send(*qg_copy(s))
        return carry

    lax.fori_loop(0, HEADS, start_qg, 0)

    def to_side(p, c, side):
        row = p // 2 * 3 + p % 2 + half
        i = p * PARTS + c
        return remote(
            kv_ref.at[1, row, c], kv_ref.at[2 - 2 * side, row, c], side_sent.at[side, i], side_sem.at[1 - side, i],
            z * WC + w + 2 * side - 1, g,
        )

    def to_core(p, c, col):
        i = p // 2 * PARTS + c
        return remote(
            kv_ref.at[col, p // 2 * 3 + 1, c], kv_ref.at[col, p // 2 * 3 + 2 * half, c],
            core_sent.at[col, i], core_sem.at[col, i], z * WC + w, g + 1 - 2 * half,
        )

    def here(ref, arrived_sem):
        return pltpu.make_async_copy(ref, ref, arrived_sem)

    def near(side):
        return w > 0 if side == 0 else w < WC - 1

    @pl.when(busy)
    def _():
        first = (4 * head + 3) // 3

        def forward(i, carry):
            lin = (first - i + 16) % 16
            c, p = lin // 4, lin % 4
            here(kv_ref.at[1, p // 2 * 3 + p % 2 + half, c], kv_sem.at[p * PARTS + c]).wait()
            for side in (0, 1):

                @pl.when(near(side))
                def _():
                    to_side(p, c, side).start()

            @pl.when(p % 2 + half == 1)
            def _():
                to_core(p, c, 1).start()

            return carry

        lax.fori_loop(0, 16, forward, 0)

        def side_in(i, carry):
            lin = (first - i + 16) % 16
            c, p = lin // 4, lin % 4
            for side in (0, 1):

                @pl.when(near(side))
                def _():
                    here(kv_ref.at[2 * side, p // 2 * 3 + p % 2 + half, c], side_sem.at[side, p * PARTS + c]).wait()

                    @pl.when(p % 2 + half == 1)
                    def _():
                        to_core(p, c, 2 * side).start()

            return carry

        lax.fori_loop(0, 16, side_in, 0)

        def arrive(i, carry):
            p, c = i // PARTS, i % PARTS
            here(qg_ref.at[p, c], qg_sem.at[i]).wait()
            for side in (0, 1):

                @pl.when(near(side))
                def _():
                    to_side(p, c, side).wait_send()

            return carry

        lax.fori_loop(0, 16, arrive, 0)

        def core_in(i, carry):
            p, c = i // PARTS * 2, i % PARTS

            def both(col):
                here(kv_ref.at[col, i // PARTS * 3 + 2 * (1 - half), c], core_sem.at[col, i]).wait()
                to_core(p, c, col).wait_send()

            both(1)
            for side in (0, 1):

                @pl.when(near(side))
                def _():
                    both(2 * side)

            return carry

        lax.fori_loop(0, 2 * PARTS, core_in, 0)

    def finish(s, carry):
        sent(*kv_copy(s))
        sent(*qg_copy(s))
        return carry

    lax.fori_loop(0, HEADS, finish, 0)


def spread(q, k, v, o, g, mask):
    vmem = pl.BlockSpec(memory_space=pltpu.VMEM)
    hbm = pl.BlockSpec(memory_space=pl.ANY)
    sem = pltpu.SemaphoreType.DMA
    return pl.pallas_call(
        spread_kernel,
        out_shape=(
            jax.ShapeDtypeStruct((3, 6, PARTS, 2, PIECE, HDIM), BF16),
            jax.ShapeDtypeStruct((4, PARTS, ROWS, HDIM), BF16),
        ),
        in_specs=[hbm] * 5 + [vmem],
        out_specs=(hbm, hbm),
        scratch_shapes=[
            pltpu.VMEM((5, PIECE, HEADS * HDIM), BF16),
            pltpu.VMEM((HEADS, 2, PIECE, HDIM), BF16),
            pltpu.VMEM((HEADS, ROWS, HDIM), BF16),
            sem((5,)),
            sem((HEADS,)),
            sem((HEADS,)),
            sem((16,)),
            sem((16,)),
            sem((2, 16)),
            sem((2, 16)),
            sem((3, 2 * PARTS)),
            sem((3, 2 * PARTS)),
        ],
        compiler_params=pltpu.CompilerParams(
            collective_id=0, has_side_effects=True, vmem_limit_bytes=60 * 1024 * 1024
        ),
    )(q, k, v, o, g, mask)


def dot(a, b, dims):
    return lax.dot_general(a, b, (dims, ((), ())), preferred_element_type=F32)


def attend_kernel(
    kv_any, qg_any,
    own_ref, halo_ref, outer_ref, inner_ref,
    kv_ref, qg_ref, load_sem, weights, top, total, alpha, query_t, terms, active, counts, queries_t, grads_t,
):
    z, w, g = place()
    busy, _, half = item_here(z, g)

    @pl.when(busy)
    def _():
        loads = [
            pltpu.make_async_copy(qg_any, qg_ref, load_sem.at[0]),
            pltpu.make_async_copy(kv_any.at[1], kv_ref.at[1], load_sem.at[1]),
            pltpu.make_async_copy(kv_any.at[0], kv_ref.at[0], load_sem.at[2]),
            pltpu.make_async_copy(kv_any.at[2], kv_ref.at[2], load_sem.at[3]),
        ]
        for load in loads:
            load.start()
        terms[...] = jnp.zeros(terms.shape, F32)
        for load in loads[:2]:
            load.wait()

        for q in range(4):
            t = q // 2
            flags = qg_ref[q, 0, 2 * PIECE :].astype(F32)[3:4]
            bit = lax.broadcasted_iota(jnp.int32, (1, HDIM), 1) - 9 * (1 - t)
            inside = jnp.logical_and(bit >= 0, bit < 18)
            power = jnp.where(inside, jnp.left_shift(1, jnp.clip(bit, 0, 17)), 0)
            bits = jnp.sum(power.astype(F32) * flags).astype(jnp.int32)
            count = jnp.int32(0)
            for n in range(18):
                col, time2, row2 = n // 6, n % 6 // 3, n % 3
                for up in (-1, 0, 1):
                    if not 0 <= row2 - up - q % 2 <= 1 or (up == 0 and time2 == t and col == 1):
                        continue
                    entry = time2 * 9 + (up + 1) * 3 + col
                    kept = jnp.logical_and((bits >> entry) % 2 == 1, half == row2 - up - q % 2)
                    if col != 1:
                        kept = jnp.logical_and(kept, w > 0 if col == 0 else w < WC - 1)
                    active[q, count] = n
                    count = count + jnp.where(kept, 1, 0)
            counts[q] = count

        def query(q, carry):
            t, row = q // 2, q % 2 + half
            queries = qg_ref[q, :, :PIECE].reshape(TILE, HDIM)
            grads = qg_ref[q, :, PIECE : 2 * PIECE].reshape(TILE, HDIM)
            rest = qg_ref[q, :, 2 * PIECE :].astype(F32)
            deltas = rest[:, 0:1, :PIECE] + rest[:, 1:2, :PIECE] + rest[:, 2:3, :PIECE]
            delta = jnp.concatenate([deltas[c] for c in range(PARTS)], axis=1)
            query_t[...] = jnp.zeros((HDIM, TILE), F32)
            centre = 6 + 3 * t + row
            count = counts[q]

            def keys_of(n):
                return kv_ref[n // 6, n % 6, :, 0].reshape(TILE, HDIM)

            queries_t[...] = queries.T

            def score(n):
                return dot(keys_of(n), queries_t[...], ((1,), (0,))) * (SCALE * LOG2E)

            own = score(centre)
            first = jnp.max(own, axis=0, keepdims=True)
            top[...] = first
            own = jnp.exp2(own - first)
            weights[centre] = own
            total[...] = jnp.sum(own.reshape(-1, 8, TILE), axis=0)

            @pl.when(q == 0)
            def _():
                for load in loads[2:]:
                    load.wait()


            grads_t[...] = grads.T

            def scores(ns):
                keys = jnp.concatenate([keys_of(n) for n in ns], axis=0)
                e = jnp.exp2(dot(keys, queries_t[...], ((1,), (0,))) * (SCALE * LOG2E) - top[...])
                for m, n in enumerate(ns):
                    weights[n] = e[m * TILE : (m + 1) * TILE]
                total[...] += jnp.sum(e.reshape(-1, 8, TILE), axis=0)

            def in_groups(step):
                done = 0
                for size in GROUPS:

                    def some(i, carry, size=size, done=done):
                        step([active[q, done + size * i + m] for m in range(size)])
                        return carry

                    rounds = (count - done) // size
                    lax.fori_loop(0, rounds, some, 0)
                    done = done + rounds * size

            in_groups(scores)

            @pl.when(jnp.logical_not(jnp.max(total[...]) < 2.0**100))
            def _():
                def higher(i, carry):
                    top[...] = jnp.maximum(top[...], jnp.max(score(active[q, i]), axis=0, keepdims=True))
                    return carry

                def again(i, carry):
                    scores([active[q, i]])
                    return carry

                lax.fori_loop(0, count, higher, 0)
                total[...] = jnp.zeros((8, TILE), F32)
                scores([centre])
                lax.fori_loop(0, count, again, 0)

            alpha[...] = 1.0 / jnp.sum(total[...], axis=0, keepdims=True)

            def grad_terms(ns):
                values = jnp.concatenate([kv_ref[n // 6, n % 6, :, 1].reshape(TILE, HDIM) for n in ns], axis=0)
                probs = jnp.concatenate([weights[n] for n in ns], axis=0) * alpha[...]
                prob_grads = dot(values, grads_t[...], ((1,), (0,)))
                score_grads = (probs * (prob_grads - delta)).astype(BF16)
                key_terms = dot(score_grads, queries, ((1,), (0,)))
                value_terms = dot(probs.astype(BF16), grads, ((1,), (0,)))
                for m, n in enumerate(ns):
                    terms[n, 0] += key_terms[m * TILE : (m + 1) * TILE]
                    terms[n, 1] += value_terms[m * TILE : (m + 1) * TILE]
                keys = jnp.concatenate([keys_of(n) for n in ns], axis=0)
                query_t[...] += dot(keys, score_grads, ((0,), (0,)))

            grad_terms([centre])
            in_groups(grad_terms)
            halo_ref[3, t, :, q % 2] = (query_t[...] * SCALE).astype(BF16).T.reshape(PARTS, PIECE, HDIM)
            return carry

        lax.fori_loop(0, 4, query, 0)

        def finish(t, carry):
            for kind, scale in ((0, SCALE), (1, 1.0)):

                def term(col, row):
                    return (terms[6 * col + 3 * t + row, kind] * scale).reshape(PARTS, PIECE, HDIM)

                for col in range(3):
                    halo_ref[col, t, :, kind] = term(col, 2 * (1 - half)).astype(BF16)
                for side in (0, 1):
                    outer_ref[side, t, :, kind] = term(2 * side, 2 * half).astype(BF16)
                    inner_ref[side, t, :, kind] = term(2 * side, 1)
                for row in (0, 1):
                    own_ref[2 * t + row, :, kind] = term(1, row + half)
            return carry

        lax.fori_loop(0, 2, finish, 0)


def attend(kv, qg):
    vmem = pl.BlockSpec(memory_space=pltpu.VMEM)
    hbm = pl.BlockSpec(memory_space=pl.ANY)
    block = (PARTS, 2, PIECE, HDIM)
    return pl.pallas_call(
        attend_kernel,
        out_shape=(
            jax.ShapeDtypeStruct((4, *block), F32),
            jax.ShapeDtypeStruct((4, 2, *block), BF16),
            jax.ShapeDtypeStruct((2, 2, *block), BF16),
            jax.ShapeDtypeStruct((2, 2, *block), F32),
        ),
        in_specs=[hbm, hbm],
        out_specs=(vmem,) * 4,
        scratch_shapes=[
            pltpu.VMEM(kv.shape, BF16),
            pltpu.VMEM(qg.shape, BF16),
            pltpu.SemaphoreType.DMA((4,)),
            pltpu.VMEM((18, TILE, TILE), F32),
            pltpu.VMEM((1, TILE), F32),
            pltpu.VMEM((8, TILE), F32),
            pltpu.VMEM((1, TILE), F32),
            pltpu.VMEM((HDIM, TILE), F32),
            pltpu.VMEM((18, 2, TILE, HDIM), F32),
            pltpu.SMEM((4, 19), jnp.int32),
            pltpu.SMEM((4,), jnp.int32),
            pltpu.VMEM((HDIM, TILE), BF16),
            pltpu.VMEM((HDIM, TILE), BF16),
        ],
        compiler_params=pltpu.CompilerParams(vmem_limit_bytes=47616 * 1024),
        cost_estimate=pl.CostEstimate(flops=12_000_000_000, bytes_accessed=10_000_000, transcendentals=9_000_000),
    )(kv, qg)


def collect_kernel(
    own_any, halo_ref, outer_ref, inner_any,
    got_q, got_kv,
    own_ref, inner_ref, from_core, mixed, beside, ready,
    load_sem, core_sent, core_sem, side_sent, side_sem, q_sent, q_sem, kv_sent, kv_sem,
):
    z, w, g = place()
    loads = [
        pltpu.make_async_copy(inner_any, inner_ref, load_sem.at[0]),
        pltpu.make_async_copy(own_any, own_ref, load_sem.at[1]),
    ]
    for load in loads:
        load.start()
    barrier = greet(z, w, g)
    busy, head, half = item_here(z, g)

    @pl.when(w == 0)
    def _():
        beside[0] = jnp.zeros(beside.shape[1:], BF16)

    @pl.when(w == WC - 1)
    def _():
        beside[1] = jnp.zeros(beside.shape[1:], BF16)

    met(barrier, w)

    def near(side):
        return w > 0 if side == 0 else w < WC - 1

    def here(ref, arrived_sem):
        return pltpu.make_async_copy(ref, ref, arrived_sem)

    def to_core(t, col):
        return remote(
            halo_ref.at[col, t], from_core.at[col, t], core_sent.at[col, t], core_sem.at[col, t],
            z * WC + w, g + 1 - 2 * half,
        )

    def to_side(t, c, inner, side):
        p = 2 * t + (1 - half if inner else half)
        i = p * PARTS + c
        src = mixed.at[side, t, c] if inner else outer_ref.at[side, t, c]
        return remote(
            src, beside.at[1 - side, p, c], side_sent.at[side, i], side_sem.at[1 - side, i],
            z * WC + w + 2 * side - 1, g,
        )

    def q_copy(i):
        n = (i + 4 * z) % (4 * PARTS)
        q, c = n // PARTS, n % PARTS
        to = q // 2 * 4 + 2 * half + q % 2
        own = jnp.logical_and(to == z, c == g)
        return halo_ref.at[3, q // 2, c, q % 2], got_q.at[head], q_sent.at[n], q_sem.at[head], to * WC + w, c, own

    def kv_copy(p, c):
        to = p // 2 * 4 + p % 2 + 2 * half
        own = jnp.logical_and(to == z, c == g)
        return ready.at[p, c], got_kv.at[head], kv_sent.at[p * PARTS + c], kv_sem.at[head], to * WC + w, c, own

    @pl.when(busy)
    def _():
        for col in (0, 2, 1):
            for t in (0, 1):

                @pl.when(near(col // 2) if col != 1 else w >= 0)
                def _():
                    to_core(t, col).start()

        def outer_out(i, carry):
            for side in (0, 1):

                @pl.when(near(side))
                def _():
                    to_side(i % 2, i // 2, False, side).start()

            return carry

        lax.fori_loop(0, 2 * PARTS, outer_out, 0)

        def start_q(i, carry):
            send(*q_copy(i))
            return carry

        lax.fori_loop(0, 4 * PARTS, start_q, 0)

        for load in loads:
            load.wait()

        def add(t, c, inner):
            p = 2 * t + (1 - half if inner else half)
            for side in (0, 1):

                @pl.when(near(side))
                def _():
                    here(beside.at[side, p, c], side_sem.at[side, p * PARTS + c]).wait()

            both = own_ref[p, c] + beside[0, p, c].astype(F32) + beside[1, p, c].astype(F32)
            ready[p, c] = both.astype(BF16)
            send(*kv_copy(p, c))

        for t in (0, 1):
            for side in (0, 1):

                @pl.when(near(side))
                def _():
                    here(from_core.at[2 * side, t], core_sem.at[2 * side, t]).wait()

            def inner_out(c, carry):
                for side in (0, 1):

                    @pl.when(near(side))
                    def _():
                        both = inner_ref[side, t, c] + from_core[2 * side, t, c].astype(F32)
                        mixed[side, t, c] = both.astype(BF16)
                        to_side(t, c, True, side).start()

                return carry

            lax.fori_loop(0, PARTS, inner_out, 0)

        for t in (0, 1):
            here(from_core.at[1, t], core_sem.at[1, t]).wait()
            p = 2 * t + 1 - half
            for c in range(PARTS):
                own_ref[p, c] = own_ref[p, c] + from_core[1, t, c].astype(F32)

        def add_outer(i, carry):
            add(i % 2, i // 2, False)
            return carry

        lax.fori_loop(0, 2 * PARTS, add_outer, 0)

        def add_inner(i, carry):
            add(i // PARTS, i % PARTS, True)
            return carry

        lax.fori_loop(0, 2 * PARTS, add_inner, 0)

        for t in (0, 1):
            to_core(t, 1).wait_send()
            for side in (0, 1):

                @pl.when(near(side))
                def _():
                    to_core(t, 2 * side).wait_send()

        def side_sends(i, carry):
            for side in (0, 1):

                @pl.when(near(side))
                def _():
                    to_side(i % 2, i // 2, False, side).wait_send()
                    to_side(i % 2, i // 2, True, side).wait_send()

            return carry

        lax.fori_loop(0, 2 * PARTS, side_sends, 0)

        def finish(n, carry):
            sent(*kv_copy(n // PARTS, n % PARTS))
            sent(*q_copy(n))
            return carry

        lax.fori_loop(0, 4 * PARTS, finish, 0)

    @pl.when(jnp.logical_not(busy))
    def _():
        for load in loads:
            load.wait()

    def arrived(j, carry):
        here(got_q.at[j], q_sem.at[j]).wait()
        here(got_kv.at[j], kv_sem.at[j]).wait()
        return carry

    lax.fori_loop(0, HEADS, arrived, 0)


def collect(own, halo, outer, inner):
    vmem = pl.BlockSpec(memory_space=pltpu.VMEM)
    hbm = pl.BlockSpec(memory_space=pl.ANY)
    sem = pltpu.SemaphoreType.DMA
    block = (PARTS, 2, PIECE, HDIM)
    return pl.pallas_call(
        collect_kernel,
        out_shape=(
            jax.ShapeDtypeStruct((HEADS, PIECE, HDIM), BF16),
            jax.ShapeDtypeStruct((HEADS, 2, PIECE, HDIM), BF16),
        ),
        in_specs=[hbm] * 4,
        out_specs=(vmem, vmem),
        scratch_shapes=[
            pltpu.VMEM((4, *block), F32),
            pltpu.VMEM((2, 2, *block), F32),
            pltpu.VMEM((3, 2, *block), BF16),
            pltpu.VMEM((2, 2, *block), BF16),
            pltpu.VMEM((2, 4, *block), BF16),
            pltpu.VMEM((4, *block), BF16),
            sem((2,)),
            sem((3, 2)),
            sem((3, 2)),
            sem((2, 16)),
            sem((2, 16)),
            sem((4 * PARTS,)),
            sem((HEADS,)),
            sem((4 * PARTS,)),
            sem((HEADS,)),
        ],
        compiler_params=pltpu.CompilerParams(
            collective_id=1, has_side_effects=True, vmem_limit_bytes=47104 * 1024
        ),
    )(own, halo, outer, inner)


def lay_kernel(q_ref, kv_ref, oq_ref, ok_ref, ov_ref, sems):
    copies = []
    for j in range(HEADS):
        cols = pl.ds(j * HDIM, HDIM)
        for i, (src, dst) in enumerate(((q_ref.at[j], oq_ref), (kv_ref.at[j, 0], ok_ref), (kv_ref.at[j, 1], ov_ref))):
            copies.append(pltpu.make_async_copy(src, dst.at[:, cols], sems.at[i, j]))
    for copy in copies:
        copy.start()
    for copy in copies:
        copy.wait()


def lay(q, kv):
    vmem = pl.BlockSpec(memory_space=pltpu.VMEM)
    hbm = pl.BlockSpec(memory_space=pl.ANY)
    out = jax.ShapeDtypeStruct((PIECE, HEADS * HDIM), BF16)
    return pl.pallas_call(
        lay_kernel,
        out_shape=(out, out, out),
        in_specs=[vmem, vmem],
        out_specs=(hbm, hbm, hbm),
        scratch_shapes=[pltpu.SemaphoreType.DMA((3, HEADS))],
        compiler_params=pltpu.CompilerParams(vmem_limit_bytes=16 * 1024 * 1024),
    )(q, kv)


def shards(query_vecs, key_vecs, value_vecs, outputs, out_grads, keep_mask):
    return lay(*collect(*attend(*spread(query_vecs, key_vecs, value_vecs, outputs, out_grads, keep_mask))))


def solution(mesh):
    rows = P(("tile", "head"), None)
    return jax.shard_map(
        shards,
        mesh=mesh,
        in_specs=(rows, rows, rows, rows, rows, P("tile", None)),
        out_specs=(rows, rows, rows),
        check_vma=False,
    )
```

```python
import jax
import jax.numpy as jnp
from jax import lax
from jax.experimental import pallas as pl
from jax.experimental.pallas import tpu as pltpu
from jax.sharding import PartitionSpec as P

MESH = pl.DeviceIdType.MESH
HEADS = 12
HDIM = 128
PIECE = 96
PARTS = 4
TILE = PIECE * PARTS
ROWS = 2 * PIECE + 16
WC = 8
GROUPS = (6, 4, 3, 2, 1)
ZC = 8
SCALE = HDIM**-0.5
LOG2E = 1.4426950408889634
F32 = jnp.float32
BF16 = jnp.bfloat16


def place():
    tile = lax.axis_index("tile")
    return tile // WC, tile % WC, lax.axis_index("head")


def item_here(z, g):
    r = (z - 2 * (g // 2) + ZC) % ZC
    return r % 4 != 0, 6 * (g // 2) + r % 4 - 1 + 3 * (r // 4), g % 2


def item_z(head):
    k = head % 6
    return (k % 3 + 1 + 4 * (k // 3) + 2 * (head // 6)) % ZC


def greet(z, w, g):
    barrier = pltpu.get_barrier_semaphore()

    def hello(i, carry):
        zz, gg = i // PARTS, i % PARTS

        @pl.when(jnp.logical_or(zz != z, gg != g))
        def _():
            pl.semaphore_signal(barrier, inc=1, device_id=(zz * WC + w, gg), device_id_type=MESH)

        return carry

    lax.fori_loop(0, ZC * PARTS, hello, 0)

    @pl.when(w > 0)
    def _():
        pl.semaphore_signal(barrier, inc=1, device_id=(z * WC + w - 1, g), device_id_type=MESH)

    @pl.when(w < WC - 1)
    def _():
        pl.semaphore_signal(barrier, inc=1, device_id=(z * WC + w + 1, g), device_id_type=MESH)

    return barrier


def met(barrier, w):
    beside = jnp.where(jnp.logical_or(w == 0, w == WC - 1), 1, 2)
    pl.semaphore_wait(barrier, ZC * PARTS - 1 + beside)


def remote(src, dst, send_sem, recv_sem, tile, head):
    return pltpu.make_async_remote_copy(
        src_ref=src, dst_ref=dst, send_sem=send_sem, recv_sem=recv_sem, device_id=(tile, head), device_id_type=MESH
    )


def send(src, dst, send_sem, recv_sem, tile, head, own):
    @pl.when(own)
    def _():
        pltpu.make_async_copy(src, dst, recv_sem).start()

    @pl.when(jnp.logical_not(own))
    def _():
        remote(src, dst, send_sem, recv_sem, tile, head).start()


def sent(src, dst, send_sem, recv_sem, tile, head, own):
    @pl.when(jnp.logical_not(own))
    def _():
        remote(src, dst, send_sem, recv_sem, tile, head).wait_send()


def spread_kernel(
    q_ref, k_ref, v_ref, o_ref, g_ref, mask_ref,
    kv_ref, qg_ref,
    given, kv_out, qg_out,
    given_sem, kv_sent, qg_sent, kv_sem, qg_sem, side_sent, side_sem, core_sent, core_sem,
):
    z, w, g = place()
    loads = [pltpu.make_async_copy(ref, given.at[i], given_sem.at[i]) for i, ref in enumerate((k_ref, v_ref, q_ref, g_ref, o_ref))]
    for load in loads:
        load.start()
    barrier = greet(z, w, g)
    busy, head, half = item_here(z, g)
    t, h = z // 4, z % 4
    to_half, qslot = h // 2, z // 4 * 2 + h % 2
    slot = t * 3 + h - to_half
    source = g * 4 + qslot
    base = 3 * source // 4

    for i, load in enumerate(loads[:2]):
        load.wait()
        for j in range(HEADS):
            kv_out[j, i] = given[i, :, j * HDIM : (j + 1) * HDIM]

    met(barrier, w)

    def target(s):
        j = (base + s) % HEADS
        zj, gj = item_z(j), 2 * (j // 6) + to_half
        return j, zj * WC + w, gj, jnp.logical_and(zj == z, gj == g)

    def kv_copy(s):
        j, tile, gj, own = target(s)
        return kv_out.at[j], kv_ref.at[1, slot, g], kv_sent.at[j], kv_sem.at[qslot * PARTS + g], tile, gj, own

    def qg_copy(s):
        j, tile, gj, own = target(s)
        return qg_out.at[j], qg_ref.at[qslot, g], qg_sent.at[j], qg_sem.at[qslot * PARTS + g], tile, gj, own

    def start_kv(s, carry):
        send(*kv_copy(s))
        return carry

    lax.fori_loop(0, HEADS, start_kv, 0)

    kept = mask_ref[...].astype(F32)
    kept = jnp.concatenate([kept, jnp.zeros((1, HDIM - kept.shape[1]), F32)], axis=1)
    for load in loads[2:]:
        load.wait()
    for j in range(HEADS):
        cols = slice(j * HDIM, (j + 1) * HDIM)
        grad = given[3, :, cols]
        prod = grad.astype(F32) * given[4, :, cols].astype(F32)
        prod = jnp.concatenate([prod, jnp.zeros((HDIM - PIECE, HDIM), F32)], axis=0)
        delta = jnp.sum(prod.T, axis=0, keepdims=True)
        high = delta.astype(BF16).astype(F32)
        middle = (delta - high).astype(BF16).astype(F32)
        low = delta - high - middle
        rest = jnp.concatenate([high, middle, low, kept, jnp.zeros((12, HDIM), F32)], axis=0)
        qg_out[j, :PIECE] = given[2, :, cols]
        qg_out[j, PIECE : 2 * PIECE] = grad
        qg_out[j, 2 * PIECE :] = rest.astype(BF16)

    def start_qg(s, carry):
        send(*qg_copy(s))
        return carry

    lax.fori_loop(0, HEADS, start_qg, 0)

    def to_side(p, c, side):
        row = p // 2 * 3 + p % 2 + half
        i = p * PARTS + c
        return remote(
            kv_ref.at[1, row, c], kv_ref.at[2 - 2 * side, row, c], side_sent.at[side, i], side_sem.at[1 - side, i],
            z * WC + w + 2 * side - 1, g,
        )

    def to_core(p, c, col):
        i = p // 2 * PARTS + c
        return remote(
            kv_ref.at[col, p // 2 * 3 + 1, c], kv_ref.at[col, p // 2 * 3 + 2 * half, c],
            core_sent.at[col, i], core_sem.at[col, i], z * WC + w, g + 1 - 2 * half,
        )

    def here(ref, arrived_sem):
        return pltpu.make_async_copy(ref, ref, arrived_sem)

    def near(side):
        return w > 0 if side == 0 else w < WC - 1

    @pl.when(busy)
    def _():
        first = (4 * head + 3) // 3

        def forward(i, carry):
            lin = (first - i + 16) % 16
            c, p = lin // 4, lin % 4
            here(kv_ref.at[1, p // 2 * 3 + p % 2 + half, c], kv_sem.at[p * PARTS + c]).wait()
            for side in (0, 1):

                @pl.when(near(side))
                def _():
                    to_side(p, c, side).start()

            @pl.when(p % 2 + half == 1)
            def _():
                to_core(p, c, 1).start()

            return carry

        lax.fori_loop(0, 16, forward, 0)

        def side_in(i, carry):
            lin = (first - i + 16) % 16
            c, p = lin // 4, lin % 4
            for side in (0, 1):

                @pl.when(near(side))
                def _():
                    here(kv_ref.at[2 * side, p // 2 * 3 + p % 2 + half, c], side_sem.at[side, p * PARTS + c]).wait()

                    @pl.when(p % 2 + half == 1)
                    def _():
                        to_core(p, c, 2 * side).start()

            return carry

        lax.fori_loop(0, 16, side_in, 0)

        def arrive(i, carry):
            p, c = i // PARTS, i % PARTS
            here(qg_ref.at[p, c], qg_sem.at[i]).wait()
            for side in (0, 1):

                @pl.when(near(side))
                def _():
                    to_side(p, c, side).wait_send()

            return carry

        lax.fori_loop(0, 16, arrive, 0)

        def core_in(i, carry):
            p, c = i // PARTS * 2, i % PARTS

            def both(col):
                here(kv_ref.at[col, i // PARTS * 3 + 2 * (1 - half), c], core_sem.at[col, i]).wait()
                to_core(p, c, col).wait_send()

            both(1)
            for side in (0, 1):

                @pl.when(near(side))
                def _():
                    both(2 * side)

            return carry

        lax.fori_loop(0, 2 * PARTS, core_in, 0)

    def finish(s, carry):
        sent(*kv_copy(s))
        sent(*qg_copy(s))
        return carry

    lax.fori_loop(0, HEADS, finish, 0)


def spread(q, k, v, o, g, mask):
    vmem = pl.BlockSpec(memory_space=pltpu.VMEM)
    hbm = pl.BlockSpec(memory_space=pl.ANY)
    sem = pltpu.SemaphoreType.DMA
    return pl.pallas_call(
        spread_kernel,
        out_shape=(
            jax.ShapeDtypeStruct((3, 6, PARTS, 2, PIECE, HDIM), BF16),
            jax.ShapeDtypeStruct((4, PARTS, ROWS, HDIM), BF16),
        ),
        in_specs=[hbm] * 5 + [vmem],
        out_specs=(hbm, hbm),
        scratch_shapes=[
            pltpu.VMEM((5, PIECE, HEADS * HDIM), BF16),
            pltpu.VMEM((HEADS, 2, PIECE, HDIM), BF16),
            pltpu.VMEM((HEADS, ROWS, HDIM), BF16),
            sem((5,)),
            sem((HEADS,)),
            sem((HEADS,)),
            sem((16,)),
            sem((16,)),
            sem((2, 16)),
            sem((2, 16)),
            sem((3, 2 * PARTS)),
            sem((3, 2 * PARTS)),
        ],
        compiler_params=pltpu.CompilerParams(
            collective_id=0, has_side_effects=True, vmem_limit_bytes=60 * 1024 * 1024
        ),
    )(q, k, v, o, g, mask)


def dot(a, b, dims):
    return lax.dot_general(a, b, (dims, ((), ())), preferred_element_type=F32)


def attend_kernel(
    kv_any, qg_any,
    own_ref, halo_ref, outer_ref, inner_ref,
    kv_ref, qg_ref, load_sem, weights, top, total, alpha, query_t, terms, active, counts, queries_t, grads_t,
):
    z, w, g = place()
    busy, _, half = item_here(z, g)

    @pl.when(busy)
    def _():
        loads = [
            pltpu.make_async_copy(qg_any, qg_ref, load_sem.at[0]),
            pltpu.make_async_copy(kv_any.at[1], kv_ref.at[1], load_sem.at[1]),
            pltpu.make_async_copy(kv_any.at[0], kv_ref.at[0], load_sem.at[2]),
            pltpu.make_async_copy(kv_any.at[2], kv_ref.at[2], load_sem.at[3]),
        ]
        for load in loads:
            load.start()
        terms[...] = jnp.zeros(terms.shape, F32)
        for load in loads[:2]:
            load.wait()

        for q in range(4):
            t = q // 2
            flags = qg_ref[q, 0, 2 * PIECE :].astype(F32)[3:4]
            bit = lax.broadcasted_iota(jnp.int32, (1, HDIM), 1) - 9 * (1 - t)
            inside = jnp.logical_and(bit >= 0, bit < 18)
            power = jnp.where(inside, jnp.left_shift(1, jnp.clip(bit, 0, 17)), 0)
            bits = jnp.sum(power.astype(F32) * flags).astype(jnp.int32)
            count = jnp.int32(0)
            for n in range(18):
                col, time2, row2 = n // 6, n % 6 // 3, n % 3
                for up in (-1, 0, 1):
                    if not 0 <= row2 - up - q % 2 <= 1 or (up == 0 and time2 == t and col == 1):
                        continue
                    entry = time2 * 9 + (up + 1) * 3 + col
                    kept = jnp.logical_and((bits >> entry) % 2 == 1, half == row2 - up - q % 2)
                    if col != 1:
                        kept = jnp.logical_and(kept, w > 0 if col == 0 else w < WC - 1)
                    active[q, count] = n
                    count = count + jnp.where(kept, 1, 0)
            counts[q] = count

        def query(q, carry):
            t, row = q // 2, q % 2 + half
            queries = qg_ref[q, :, :PIECE].reshape(TILE, HDIM)
            grads = qg_ref[q, :, PIECE : 2 * PIECE].reshape(TILE, HDIM)
            rest = qg_ref[q, :, 2 * PIECE :].astype(F32)
            deltas = rest[:, 0:1, :PIECE] + rest[:, 1:2, :PIECE] + rest[:, 2:3, :PIECE]
            delta = jnp.concatenate([deltas[c] for c in range(PARTS)], axis=1)
            query_t[...] = jnp.zeros((HDIM, TILE), F32)
            centre = 6 + 3 * t + row
            count = counts[q]

            def keys_of(n):
                return kv_ref[n // 6, n % 6, :, 0].reshape(TILE, HDIM)

            queries_t[...] = queries.T

            def score(n):
                return dot(keys_of(n), queries_t[...], ((1,), (0,))) * (SCALE * LOG2E)

            own = score(centre)
            first = jnp.max(own, axis=0, keepdims=True)
            top[...] = first
            own = jnp.exp2(own - first)
            weights[centre] = own
            total[...] = jnp.sum(own.reshape(-1, 8, TILE), axis=0)

            @pl.when(q == 0)
            def _():
                for load in loads[2:]:
                    load.wait()


            grads_t[...] = grads.T

            def scores(ns):
                keys = jnp.concatenate([keys_of(n) for n in ns], axis=0)
                e = jnp.exp2(dot(keys, queries_t[...], ((1,), (0,))) * (SCALE * LOG2E) - top[...])
                for m, n in enumerate(ns):
                    weights[n] = e[m * TILE : (m + 1) * TILE]
                total[...] += jnp.sum(e.reshape(-1, 8, TILE), axis=0)

            def in_groups(step):
                done = 0
                for size in GROUPS:

                    def some(i, carry, size=size, done=done):
                        step([active[q, done + size * i + m] for m in range(size)])
                        return carry

                    rounds = (count - done) // size
                    lax.fori_loop(0, rounds, some, 0)
                    done = done + rounds * size

            in_groups(scores)

            @pl.when(jnp.logical_not(jnp.max(total[...]) < 2.0**100))
            def _():
                def higher(i, carry):
                    top[...] = jnp.maximum(top[...], jnp.max(score(active[q, i]), axis=0, keepdims=True))
                    return carry

                def again(i, carry):
                    scores([active[q, i]])
                    return carry

                lax.fori_loop(0, count, higher, 0)
                total[...] = jnp.zeros((8, TILE), F32)
                scores([centre])
                lax.fori_loop(0, count, again, 0)

            alpha[...] = 1.0 / jnp.sum(total[...], axis=0, keepdims=True)

            def grad_terms(ns):
                values = jnp.concatenate([kv_ref[n // 6, n % 6, :, 1].reshape(TILE, HDIM) for n in ns], axis=0)
                probs = jnp.concatenate([weights[n] for n in ns], axis=0) * alpha[...]
                prob_grads = dot(values, grads_t[...], ((1,), (0,)))
                score_grads = (probs * (prob_grads - delta)).astype(BF16)
                key_terms = dot(score_grads, queries, ((1,), (0,)))
                value_terms = dot(probs.astype(BF16), grads, ((1,), (0,)))
                for m, n in enumerate(ns):
                    terms[n, 0] += key_terms[m * TILE : (m + 1) * TILE]
                    terms[n, 1] += value_terms[m * TILE : (m + 1) * TILE]
                keys = jnp.concatenate([keys_of(n) for n in ns], axis=0)
                query_t[...] += dot(keys, score_grads, ((0,), (0,)))

            grad_terms([centre])
            in_groups(grad_terms)
            halo_ref[3, t, :, q % 2] = (query_t[...] * SCALE).astype(BF16).T.reshape(PARTS, PIECE, HDIM)
            return carry

        lax.fori_loop(0, 4, query, 0)

        def finish(t, carry):
            for kind, scale in ((0, SCALE), (1, 1.0)):

                def term(col, row):
                    return (terms[6 * col + 3 * t + row, kind] * scale).reshape(PARTS, PIECE, HDIM)

                for col in range(3):
                    halo_ref[col, t, :, kind] = term(col, 2 * (1 - half)).astype(BF16)
                for side in (0, 1):
                    outer_ref[side, t, :, kind] = term(2 * side, 2 * half).astype(BF16)
                    inner_ref[side, t, :, kind] = term(2 * side, 1)
                for row in (0, 1):
                    own_ref[2 * t + row, :, kind] = term(1, row + half)
            return carry

        lax.fori_loop(0, 2, finish, 0)


def attend(kv, qg):
    vmem = pl.BlockSpec(memory_space=pltpu.VMEM)
    hbm = pl.BlockSpec(memory_space=pl.ANY)
    block = (PARTS, 2, PIECE, HDIM)
    return pl.pallas_call(
        attend_kernel,
        out_shape=(
            jax.ShapeDtypeStruct((4, *block), F32),
            jax.ShapeDtypeStruct((4, 2, *block), BF16),
            jax.ShapeDtypeStruct((2, 2, *block), BF16),
            jax.ShapeDtypeStruct((2, 2, *block), F32),
        ),
        in_specs=[hbm, hbm],
        out_specs=(vmem,) * 4,
        scratch_shapes=[
            pltpu.VMEM(kv.shape, BF16),
            pltpu.VMEM(qg.shape, BF16),
            pltpu.SemaphoreType.DMA((4,)),
            pltpu.VMEM((18, TILE, TILE), F32),
            pltpu.VMEM((1, TILE), F32),
            pltpu.VMEM((8, TILE), F32),
            pltpu.VMEM((1, TILE), F32),
            pltpu.VMEM((HDIM, TILE), F32),
            pltpu.VMEM((18, 2, TILE, HDIM), F32),
            pltpu.SMEM((4, 19), jnp.int32),
            pltpu.SMEM((4,), jnp.int32),
            pltpu.VMEM((HDIM, TILE), BF16),
            pltpu.VMEM((HDIM, TILE), BF16),
        ],
        compiler_params=pltpu.CompilerParams(vmem_limit_bytes=47616 * 1024),
        cost_estimate=pl.CostEstimate(flops=12_000_000_000, bytes_accessed=10_000_000, transcendentals=9_000_000),
    )(kv, qg)


def collect_kernel(
    own_any, halo_ref, outer_ref, inner_any,
    got_q, got_kv,
    own_ref, inner_ref, from_core, mixed, beside, ready,
    load_sem, core_sent, core_sem, side_sent, side_sem, q_sent, q_sem, kv_sent, kv_sem,
):
    z, w, g = place()
    loads = [
        pltpu.make_async_copy(inner_any, inner_ref, load_sem.at[0]),
        pltpu.make_async_copy(own_any, own_ref, load_sem.at[1]),
    ]
    for load in loads:
        load.start()
    barrier = greet(z, w, g)
    busy, head, half = item_here(z, g)

    @pl.when(w == 0)
    def _():
        beside[0] = jnp.zeros(beside.shape[1:], BF16)

    @pl.when(w == WC - 1)
    def _():
        beside[1] = jnp.zeros(beside.shape[1:], BF16)

    met(barrier, w)

    def near(side):
        return w > 0 if side == 0 else w < WC - 1

    def here(ref, arrived_sem):
        return pltpu.make_async_copy(ref, ref, arrived_sem)

    def to_core(t, col):
        return remote(
            halo_ref.at[col, t], from_core.at[col, t], core_sent.at[col, t], core_sem.at[col, t],
            z * WC + w, g + 1 - 2 * half,
        )

    def to_side(t, c, inner, side):
        p = 2 * t + (1 - half if inner else half)
        i = p * PARTS + c
        src = mixed.at[side, t, c] if inner else outer_ref.at[side, t, c]
        return remote(
            src, beside.at[1 - side, p, c], side_sent.at[side, i], side_sem.at[1 - side, i],
            z * WC + w + 2 * side - 1, g,
        )

    def q_copy(i):
        n = (i + 4 * z) % (4 * PARTS)
        q, c = n // PARTS, n % PARTS
        to = q // 2 * 4 + 2 * half + q % 2
        own = jnp.logical_and(to == z, c == g)
        return halo_ref.at[3, q // 2, c, q % 2], got_q.at[head], q_sent.at[n], q_sem.at[head], to * WC + w, c, own

    def kv_copy(p, c):
        to = p // 2 * 4 + p % 2 + 2 * half
        own = jnp.logical_and(to == z, c == g)
        return ready.at[p, c], got_kv.at[head], kv_sent.at[p * PARTS + c], kv_sem.at[head], to * WC + w, c, own

    @pl.when(busy)
    def _():
        for col in (0, 2, 1):
            for t in (0, 1):

                @pl.when(near(col // 2) if col != 1 else w >= 0)
                def _():
                    to_core(t, col).start()

        def outer_out(i, carry):
            for side in (0, 1):

                @pl.when(near(side))
                def _():
                    to_side(i % 2, i // 2, False, side).start()

            return carry

        lax.fori_loop(0, 2 * PARTS, outer_out, 0)

        def start_q(i, carry):
            send(*q_copy(i))
            return carry

        lax.fori_loop(0, 4 * PARTS, start_q, 0)

        for load in loads:
            load.wait()

        def add(t, c, inner):
            p = 2 * t + (1 - half if inner else half)
            for side in (0, 1):

                @pl.when(near(side))
                def _():
                    here(beside.at[side, p, c], side_sem.at[side, p * PARTS + c]).wait()

            both = own_ref[p, c] + beside[0, p, c].astype(F32) + beside[1, p, c].astype(F32)
            ready[p, c] = both.astype(BF16)
            send(*kv_copy(p, c))

        for t in (0, 1):
            for side in (0, 1):

                @pl.when(near(side))
                def _():
                    here(from_core.at[2 * side, t], core_sem.at[2 * side, t]).wait()

            def inner_out(c, carry):
                for side in (0, 1):

                    @pl.when(near(side))
                    def _():
                        both = inner_ref[side, t, c] + from_core[2 * side, t, c].astype(F32)
                        mixed[side, t, c] = both.astype(BF16)
                        to_side(t, c, True, side).start()

                return carry

            lax.fori_loop(0, PARTS, inner_out, 0)

        def add_outer(i, carry):
            add(i % 2, i // 2, False)
            return carry

        lax.fori_loop(0, 2 * PARTS, add_outer, 0)

        for t in (0, 1):
            here(from_core.at[1, t], core_sem.at[1, t]).wait()
            p = 2 * t + 1 - half
            for c in range(PARTS):
                own_ref[p, c] = own_ref[p, c] + from_core[1, t, c].astype(F32)

        def add_inner(i, carry):
            add(i // PARTS, i % PARTS, True)
            return carry

        lax.fori_loop(0, 2 * PARTS, add_inner, 0)

        for t in (0, 1):
            to_core(t, 1).wait_send()
            for side in (0, 1):

                @pl.when(near(side))
                def _():
                    to_core(t, 2 * side).wait_send()

        def side_sends(i, carry):
            for side in (0, 1):

                @pl.when(near(side))
                def _():
                    to_side(i % 2, i // 2, False, side).wait_send()
                    to_side(i % 2, i // 2, True, side).wait_send()

            return carry

        lax.fori_loop(0, 2 * PARTS, side_sends, 0)

        def finish(n, carry):
            sent(*kv_copy(n // PARTS, n % PARTS))
            sent(*q_copy(n))
            return carry

        lax.fori_loop(0, 4 * PARTS, finish, 0)

    @pl.when(jnp.logical_not(busy))
    def _():
        for load in loads:
            load.wait()

    def arrived(j, carry):
        here(got_q.at[j], q_sem.at[j]).wait()
        here(got_kv.at[j], kv_sem.at[j]).wait()
        return carry

    lax.fori_loop(0, HEADS, arrived, 0)


def collect(own, halo, outer, inner):
    vmem = pl.BlockSpec(memory_space=pltpu.VMEM)
    hbm = pl.BlockSpec(memory_space=pl.ANY)
    sem = pltpu.SemaphoreType.DMA
    block = (PARTS, 2, PIECE, HDIM)
    return pl.pallas_call(
        collect_kernel,
        out_shape=(
            jax.ShapeDtypeStruct((HEADS, PIECE, HDIM), BF16),
            jax.ShapeDtypeStruct((HEADS, 2, PIECE, HDIM), BF16),
        ),
        in_specs=[hbm] * 4,
        out_specs=(vmem, vmem),
        scratch_shapes=[
            pltpu.VMEM((4, *block), F32),
            pltpu.VMEM((2, 2, *block), F32),
            pltpu.VMEM((3, 2, *block), BF16),
            pltpu.VMEM((2, 2, *block), BF16),
            pltpu.VMEM((2, 4, *block), BF16),
            pltpu.VMEM((4, *block), BF16),
            sem((2,)),
            sem((3, 2)),
            sem((3, 2)),
            sem((2, 16)),
            sem((2, 16)),
            sem((4 * PARTS,)),
            sem((HEADS,)),
            sem((4 * PARTS,)),
            sem((HEADS,)),
        ],
        compiler_params=pltpu.CompilerParams(
            collective_id=1, has_side_effects=True, vmem_limit_bytes=47104 * 1024
        ),
    )(own, halo, outer, inner)


def lay_kernel(q_ref, kv_ref, oq_ref, ok_ref, ov_ref, sems):
    copies = []
    for j in range(HEADS):
        cols = pl.ds(j * HDIM, HDIM)
        for i, (src, dst) in enumerate(((q_ref.at[j], oq_ref), (kv_ref.at[j, 0], ok_ref), (kv_ref.at[j, 1], ov_ref))):
            copies.append(pltpu.make_async_copy(src, dst.at[:, cols], sems.at[i, j]))
    for copy in copies:
        copy.start()
    for copy in copies:
        copy.wait()


def lay(q, kv):
    vmem = pl.BlockSpec(memory_space=pltpu.VMEM)
    hbm = pl.BlockSpec(memory_space=pl.ANY)
    out = jax.ShapeDtypeStruct((PIECE, HEADS * HDIM), BF16)
    return pl.pallas_call(
        lay_kernel,
        out_shape=(out, out, out),
        in_specs=[vmem, vmem],
        out_specs=(hbm, hbm, hbm),
        scratch_shapes=[pltpu.SemaphoreType.DMA((3, HEADS))],
        compiler_params=pltpu.CompilerParams(vmem_limit_bytes=16 * 1024 * 1024),
    )(q, kv)


def shards(query_vecs, key_vecs, value_vecs, outputs, out_grads, keep_mask):
    return lay(*collect(*attend(*spread(query_vecs, key_vecs, value_vecs, outputs, out_grads, keep_mask))))


def solution(mesh):
    rows = P(("tile", "head"), None)
    return jax.shard_map(
        shards,
        mesh=mesh,
        in_specs=(rows, rows, rows, rows, rows, P("tile", None)),
        out_specs=(rows, rows, rows),
        check_vma=False,
    )
```
